32 devices in a mesh: ka: 8 (over z, y), gz: 4 (over x, core).
Axes of the slice: x: 2, y: 2, z: 4, core: 2. Of those that a mesh axis runs over, the one named last changes fastest.
Arguments:
- fields: float32 [8, 2, 32, 3, 25600], P('ka', None, None, None, 'gz'), may hold values from -0.25 to 0.25
- bvectors: float32 [2, 3], replicated, may hold values from -0.5 to 0.5
- gshift: int32 [8, 2, 3], replicated, may hold values from -1 to 1
Outputs:
- intersections: float32 [8, 4, 2, 32, 32], P('ka')
The draws below stay inside these ranges and needn't reach their ends.
All inputs are finite; a program needn't handle non-finite values.
Results may differ from the reference program's by a relative error of at most 0.0003.
Values sent between devices are 32-bit elements; how exact they have to be, the bound alone decides.
No kernel may reach another device: no remote copies, remote signals or barrier semaphores. Data moves between devices by JAX's collectives and lax.ppermute only.
A program may use at most 128 MiB of HBM per device.

```python
import math
import jax
import jax.numpy as jnp
from jax import lax

BANDS = 32
GX = 40
GY = 40
KX = 4
NZ = 16
CELLS = 25600
K = 8


def place_ends(entries, rng, low, largest):
    extent = entries.shape
    index_at = [jax.random.randint(jax.random.fold_in(rng, axis), (), 0, extent[axis]) for axis in range(len(extent))]
    entries = entries.at[tuple(index_at)].set(low)
    longest = extent.index(max(extent))
    index_at[longest] = (index_at[longest] + 1) % extent[longest]
    return entries.at[tuple(index_at)].set(largest)


def levels(key, dims, cuts, low, top_value):
    gain, own = 1.0, jax.random.fold_in(key, 6)
    for axis_at, shards_of in cuts:
        steps = jnp.exp(jax.random.uniform(jax.random.fold_in(own, axis_at), (shards_of,), jnp.float32, low / len(cuts), top_value / len(cuts)))
        gain = gain * jnp.repeat(steps, dims[axis_at] // shards_of).reshape([-1 if axis == axis_at else 1 for axis in range(len(dims))])
    return gain


def centred(rng, dims, spread, bound, pieces=(), kind=jnp.bfloat16):
    result = jax.random.normal(rng, dims, jnp.float32) * spread
    if len(pieces) > 0:
        result = levels(rng, dims, pieces, -0.22, 0.18) * result
    return jnp.clip(result, min=-bound, max=bound).astype(kind)


def setup_inputs(seed: int = 0) -> dict:
    key_of = jax.random.split(jax.random.key(seed), 4)
    return {
        "fields": centred(key_of[0], (K, 2, BANDS, 3, CELLS), (GY * NZ) ** -0.5, 0.25, ((0, 8), (4, 4)), jnp.float32),
        "bvectors": jnp.clip(jax.random.uniform(key_of[1], (2, 3), jnp.float32, -0.5, 0.5), -0.5, 0.5),
        "gshift": place_ends(jax.random.randint(key_of[2], (K, 2, 3), -1, 2), jax.random.fold_in(key_of[2], 1), -1, 1).astype(jnp.int32),
    }


two_pi = 2.0 * math.pi


def phase_angle(q_vector, xcoord, ycoord, zcoord, x_extent, y_extent, z_extent):
    return -two_pi * (q_vector[0] * xcoord / x_extent + q_vector[1] * ycoord / y_extent + q_vector[2] * zcoord / z_extent)


def intersection(left_field, right_field, angles):
    cosine_part = jnp.cos(angles)
    sine_part = jnp.sin(angles)
    r_real = right_field[0]
    r_imag = right_field[1]
    w_real = cosine_part * r_real - sine_part * r_imag
    w_imag = sine_part * r_real + cosine_part * r_imag
    band_count = left_field.shape[1]
    left_rows = jnp.concatenate([left_field[0].reshape(band_count, -1), left_field[1].reshape(band_count, -1)], axis=1)
    upper_rows = jnp.concatenate([w_real.reshape(band_count, -1), w_imag.reshape(band_count, -1)], axis=1)
    lower_rows = jnp.concatenate([w_imag.reshape(band_count, -1), -w_real.reshape(band_count, -1)], axis=1)
    right_rows = jnp.concatenate([upper_rows, lower_rows], axis=0)
    product = lax.dot_general(left_rows, right_rows, (((1,), (1,)), ((), ())), precision=lax.Precision.HIGHEST, preferred_element_type=jnp.float32)
    return jnp.stack([product[:, :band_count], product[:, band_count:]])


def reference(fields, bvectors, gshift):
    kpoint_count = fields.shape[0]
    cell_total = fields.shape[-1]
    cell_index = jnp.arange(cell_total, dtype=jnp.int32)
    xcoord = (cell_index % GX).astype(jnp.float32)
    ycoord = ((cell_index // GX) % GY).astype(jnp.float32)
    zcoord = (cell_index // (GX * GY)).astype(jnp.float32)
    shifts_float = gshift.astype(jnp.float32)

    def one_point(kpoint):
        plus_x = (kpoint + 1) % kpoint_count
        minus_x = (kpoint - 1 + kpoint_count) % kpoint_count
        plus_y = (kpoint + KX) % kpoint_count
        minus_y = (kpoint - KX + kpoint_count) % kpoint_count
        local_field = fields[kpoint]
        q_plus_x = bvectors[0] + shifts_float[kpoint, 0]
        q_minus_x = -(bvectors[0] + shifts_float[minus_x, 0])
        q_plus_y = bvectors[1] + shifts_float[kpoint, 1]
        q_minus_y = -(bvectors[1] + shifts_float[minus_y, 1])
        blocks = []
        for partner, q_vector in ((plus_x, q_plus_x), (minus_x, q_minus_x), (plus_y, q_plus_y), (minus_y, q_minus_y)):
            angles = phase_angle(q_vector, xcoord, ycoord, zcoord, GX, GY, NZ)
            blocks.append(intersection(local_field, fields[partner], angles))
        return jnp.stack(blocks)

    return lax.map(one_point, jnp.arange(kpoint_count, dtype=jnp.int32))
```

```python
import functools
import math

import jax
import jax.numpy as jnp
from jax import lax
from jax.experimental import pallas as pl
from jax.experimental.pallas import tpu as pltpu
from jax.sharding import PartitionSpec as P

GX = 40
GY = 40
KX = 4
LANES = 128
CHUNKS = 3

two_pi = 2.0 * math.pi


def shifted(value, axis, steps):
    count = lax.axis_size(axis)
    pairs = [(source, (source + steps) % count) for source in range(count)]
    return lax.ppermute(value, axis, pairs)


def phase_angle(q_vector, xcoord, ycoord, zcoord, x_extent, y_extent, z_extent):
    return -two_pi * (
        q_vector[0] * xcoord / x_extent
        + q_vector[1] * ycoord / y_extent
        + q_vector[2] * zcoord / z_extent
    )


class Parts:
    def __init__(self, components, cells, count):
        self.components = components
        self.count = count
        tiles = cells // LANES
        self.tiles = tiles
        self.main = tiles // count
        self.rest = tiles - self.main * count
        self.extra = -(-components * self.rest // count)
        self.units = components * self.main + self.extra

    def pieces(self, start, stop):
        runs = []
        unit = start
        while unit < stop:
            if unit < self.components * self.main:
                component, tile = divmod(unit, self.main)
                length = min(self.main - tile, stop - unit)
                runs.append((component, tile, length))
            else:
                length = 1
                runs.append((None, unit - self.components * self.main, 1))
            unit += length
        return runs

    def extra_unit(self, part, slot):
        number = slot * self.count + part
        valid = number < self.components * self.rest
        number = jnp.minimum(number, self.components * self.rest - 1)
        return number // self.rest, self.main * self.count + number % self.rest, valid

    def take(self, field, part, start, stop):
        bands = field.shape[2]
        found = []
        for component, tile, length in self.pieces(start, stop):
            if component is None:
                which, at, _ = self.extra_unit(part, tile)
                origin = (0, which, 0, at * LANES)
            else:
                origin = (0, component, 0, (part * self.main + tile) * LANES)
            found.append(lax.dynamic_slice(field, origin, (2, 1, bands, length * LANES))[:, 0])
        return found[0] if len(found) == 1 else jnp.concatenate(found, axis=2)

    def cell_index(self, part, start, stop):
        cells, valid = [], []
        lane = jnp.arange(LANES, dtype=jnp.int32)
        for component, tile, length in self.pieces(start, stop):
            if component is None:
                _, at, good = self.extra_unit(part, tile)
                cells.append(at * LANES + lane)
                valid.append(jnp.full((LANES,), 1.0, jnp.float32) * good.astype(jnp.float32))
            else:
                run = jnp.arange(length * LANES, dtype=jnp.int32)
                cells.append((part * self.main + tile) * LANES + run)
                valid.append(jnp.ones((length * LANES,), jnp.float32))
        return jnp.concatenate(cells), jnp.concatenate(valid)


def split_parts(value):
    high = value.astype(jnp.bfloat16)
    low = (value - high.astype(jnp.float32)).astype(jnp.bfloat16)
    return high, low


def chunk_kernel(count, offsets, first, *refs):
    blocks = refs[:count]
    cosine_ref, sine_ref = refs[count], refs[count + 1]
    rest = refs[count + 2 :]
    if first:
        total_ref, held, sems = rest
        before_ref = None
    else:
        before_ref, total_ref, held, sems = rest
    copies = [
        pltpu.make_async_copy(blocks[step], held.at[step], sems.at[step]) for step in range(count)
    ]
    for copy in copies:
        copy.start()
    for copy in copies:
        copy.wait()

    @pl.loop(0, count)
    def _(step):
        left = held[step]
        bands, cells = left.shape[1], left.shape[2]
        left_high, left_low = split_parts(left.reshape(2 * bands, cells))
        left_rows = jnp.concatenate([left_high, left_low], axis=0)
        highs, lows = [], []
        for direction, offset in enumerate(offsets):
            right = held[lax.rem(step + offset, count)]
            cosine = cosine_ref[step * len(offsets) + direction]
            sine = sine_ref[step * len(offsets) + direction]
            w_real = cosine * right[0] - sine * right[1]
            w_imag = sine * right[0] + cosine * right[1]
            high, low = split_parts(jnp.concatenate([w_real, w_imag], axis=0))
            highs.append(high)
            lows.append(low)
        right_rows = jnp.concatenate(highs + lows, axis=0)
        product = lax.dot_general(
            left_rows,
            right_rows,
            (((1,), (1,)), ((), ())),
            preferred_element_type=jnp.float32,
        )
        half = product.shape[1] // 2
        rows = product[: 2 * bands] + product[2 * bands :]
        summed = rows[:, :half] + rows[:, half:]
        if not first:
            summed = summed + before_ref[step]
        total_ref[step] = summed


def chunk_products(blocks, cosine, sine, before, offsets):
    count = len(blocks)
    _, bands, cells = blocks[0].shape
    width = 2 * len(offsets) * bands
    operands = list(blocks) + [cosine, sine]
    anywhere = pl.BlockSpec(memory_space=pl.ANY)
    inside = pl.BlockSpec(memory_space=pltpu.VMEM)
    in_specs = [anywhere] * count + [inside, inside]
    if before is not None:
        operands.append(before)
        in_specs.append(inside)
    flops = 2 * count * (4 * bands) * (2 * width) * cells
    return pl.pallas_call(
        functools.partial(chunk_kernel, count, offsets, before is None),
        out_shape=jax.ShapeDtypeStruct((count, 2 * bands, width), jnp.float32),
        in_specs=in_specs,
        out_specs=inside,
        scratch_shapes=[
            pltpu.VMEM((count, 2, bands, cells), jnp.float32),
            pltpu.SemaphoreType.DMA((count,)),
        ],
        compiler_params=pltpu.CompilerParams(vmem_limit_bytes=32 * 1024 * 1024),
        cost_estimate=pl.CostEstimate(
            flops=flops, bytes_accessed=4 * count * 2 * bands * cells, transcendentals=0
        ),
    )(*operands)


def block_factor(count):
    best = 1
    for factor in range(1, math.isqrt(count) + 1):
        if count % factor == 0:
            best = factor
    return best


def messages_kernel(count, offsets, factor, total_ref, out_ref, forward):
    me = lax.axis_index("ka")
    bands = total_ref.shape[1] // 2
    width = total_ref.shape[2]
    lane = lax.broadcasted_iota(jnp.int32, (bands, width), 1)
    real_lane = lane % (2 * bands) < bands

    @pl.loop(0, count)
    def _(step):
        with_real = total_ref[step, :bands]
        with_imag = total_ref[step, bands:]
        after = pltpu.roll(with_imag, width - bands, 1)
        ahead = pltpu.roll(with_imag, bands, 1)
        forward[step] = with_real + jnp.where(real_lane, after, -ahead)

    @pl.loop(0, count)
    def _(step):
        target = lax.rem(me + step, count)
        low = lax.rem(target, factor) + factor - lax.rem(me, factor)
        turn = lax.rem(low, factor)
        group = target // factor
        out_ref[turn, group, 0] = forward[step]
        back = jnp.zeros((bands, width), jnp.float32)
        for direction, offset in enumerate(offsets):
            other = forward[lax.rem(step + count - offset, count)]
            back = jnp.where(lane // (2 * bands) == direction, other, back)
        out_ref[turn, group, 1] = back


def messages(total, offsets, factor):
    count, rows, width = total.shape
    inside = pl.BlockSpec(memory_space=pltpu.VMEM)
    return pl.pallas_call(
        functools.partial(messages_kernel, count, offsets, factor),
        out_shape=jax.ShapeDtypeStruct((factor, count // factor, 2, rows // 2, width), jnp.float32),
        in_specs=[inside],
        out_specs=inside,
        scratch_shapes=[pltpu.VMEM((count, rows // 2, width), jnp.float32)],
    )(total)


def result_kernel(*refs):
    out_ref = refs[-1]
    total = refs[0][...]
    for ref in refs[1:-1]:
        total = total + ref[...]
    bands = out_ref.shape[2]
    flipped = total[1].T
    for direction in range(out_ref.shape[0] // 2):
        at = 2 * bands * direction
        out_ref[2 * direction, 0] = total[0, :, at : at + bands]
        out_ref[2 * direction, 1] = total[0, :, at + bands : at + 2 * bands]
        out_ref[2 * direction + 1, 0] = flipped[at : at + bands]
        out_ref[2 * direction + 1, 1] = -flipped[at + bands : at + 2 * bands]


def result(shares):
    _, bands, width = shares[0].shape
    inside = pl.BlockSpec(memory_space=pltpu.VMEM)
    return pl.pallas_call(
        result_kernel,
        out_shape=jax.ShapeDtypeStruct((width // bands, 2, bands, bands), jnp.float32),
        in_specs=[inside] * len(shares),
        out_specs=inside,
    )(*shares)


def reduced_over_points(blocks, factor):
    groups = blocks.shape[1]
    me = lax.axis_index("ka")
    count = lax.axis_size("ka")
    total = blocks[0]
    for turn in range(1, factor):
        pairs = [
            (source, source - source % factor + (source + turn) % factor) for source in range(count)
        ]
        total = total + lax.ppermute(blocks[turn], "ka", pairs)
    group = me // factor
    mine = lax.dynamic_index_in_dim(total, group, 0, keepdims=False)
    arrived = []
    for turn in range(1, groups):
        sent = lax.dynamic_index_in_dim(total, (group + turn) % groups, 0, keepdims=False)
        arrived.append(shifted(sent, "ka", turn * factor))
    return mine + sum(arrived)


def per_device(fields, bvectors, gshift):
    count = lax.axis_size("ka")
    slabs = lax.axis_size("gz")
    me = lax.axis_index("ka")
    field = fields[0].transpose(0, 2, 1, 3)
    cells = field.shape[-1]
    plane_cells = GX * GY
    slab_depth = cells // plane_cells
    z_extent = slab_depth * slabs
    parts = Parts(field.shape[1], cells, count)
    offsets = (1 % count, KX % count)

    cell_index, valid = parts.cell_index(me, 0, parts.units)
    xcoord = (cell_index % GX).astype(jnp.float32)
    ycoord = (cell_index // GX % GY).astype(jnp.float32)
    zcoord = (lax.axis_index("gz") * slab_depth + cell_index // plane_cells).astype(jnp.float32)
    shifts_float = gshift.astype(jnp.float32)
    q_vectors = jnp.roll(bvectors[None] + shifts_float, -me, axis=0).reshape(-1, 3)
    angles = phase_angle(q_vectors.T[:, :, None], xcoord, ycoord, zcoord, GX, GY, z_extent)
    cosine = (jnp.cos(angles) * valid)[:, None]
    sine = (jnp.sin(angles) * valid)[:, None]

    order = sorted(range(1, count), key=lambda step: -min(step, count - step))
    bounds = [parts.units * chunk // CHUNKS for chunk in range(CHUNKS + 1)]
    total = None
    for start, stop in zip(bounds[:-1], bounds[1:]):
        blocks = [None] * count
        for step in order:
            sent = parts.take(field, (me + count - step) % count, start, stop)
            blocks[step] = shifted(sent, "ka", -step)
        blocks[0] = parts.take(field, me, start, stop)
        lanes = slice(start * LANES, stop * LANES)
        total = chunk_products(blocks, cosine[:, :, lanes], sine[:, :, lanes], total, offsets)

    factor = block_factor(count)
    share = reduced_over_points(messages(total, offsets, factor), factor)
    shares = [share] + [shifted(share, "gz", step) for step in range(1, slabs)]
    return result(shares)[None]


def solution(mesh):
    in_specs = (P("ka", None, None, None, "gz"), P(), P())
    out_specs = P("ka", None, None, None, None)
    return jax.shard_map(
        per_device, mesh=mesh, in_specs=in_specs, out_specs=out_specs, check_vma=False
    )
```

```python
import functools
import math

import jax
import jax.numpy as jnp
from jax import lax
from jax.experimental import pallas as pl
from jax.experimental.pallas import tpu as pltpu
from jax.sharding import PartitionSpec as P

GX = 40
GY = 40
KX = 4
LANES = 128
SHARES = (0.32, 0.32, 0.26, 0.10)
AHEAD = 2

two_pi = 2.0 * math.pi


def shifted(value, axis, steps):
    count = lax.axis_size(axis)
    pairs = [(source, (source + steps) % count) for source in range(count)]
    return lax.ppermute(value, axis, pairs)


def phase_angle(q_vector, xcoord, ycoord, zcoord, x_extent, y_extent, z_extent):
    return -two_pi * (
        q_vector[0] * xcoord / x_extent
        + q_vector[1] * ycoord / y_extent
        + q_vector[2] * zcoord / z_extent
    )


def exchange(count):
    if count & (count - 1) == 0:
        half = count // 2
        turns = [turn for low in range(half) for turn in (half + low, low) if turn]
        return [functools.partial(lambda turn, me: me ^ turn, turn) for turn in turns]
    turns = sorted(range(1, count), key=lambda turn: -min(turn, count - turn))
    return [functools.partial(lambda turn, me: (me + turn) % count, turn) for turn in turns]


def exchange_back(count):
    if count & (count - 1) == 0:
        return exchange(count)
    turns = sorted(range(1, count), key=lambda turn: -min(turn, count - turn))
    return [functools.partial(lambda turn, me: (me + count - turn) % count, turn) for turn in turns]


def sent_round(value, to):
    pairs = [(source, to(source)) for source in range(lax.axis_size("ka"))]
    return lax.ppermute(value, "ka", pairs)


class Parts:
    def __init__(self, components, cells, count):
        self.components = components
        self.count = count
        tiles = cells // LANES
        self.tiles = tiles
        self.main = tiles // count
        self.rest = tiles - self.main * count
        self.extra = -(-components * self.rest // count)
        self.units = components * self.main + self.extra

    def pieces(self, start, stop):
        runs = []
        unit = start
        while unit < stop:
            if unit < self.components * self.main:
                component, tile = divmod(unit, self.main)
                length = min(self.main - tile, stop - unit)
                runs.append((component, tile, length))
            else:
                length = 1
                runs.append((None, unit - self.components * self.main, 1))
            unit += length
        return runs

    def extra_unit(self, part, slot):
        number = slot * self.count + part
        valid = number < self.components * self.rest
        number = jnp.minimum(number, self.components * self.rest - 1)
        return number // self.rest, self.main * self.count + number % self.rest, valid

    def runs(self, part, start, stop):
        found, place = [], 0
        for component, tile, length in self.pieces(start, stop):
            if component is None:
                component, at, _ = self.extra_unit(part, tile)
            else:
                at = part * self.main + tile
            found.append((component, pl.multiple_of(at * LANES, LANES), place, length * LANES))
            place += length * LANES
        return found

    def cell_index(self, part, start, stop):
        cells, valid = [], []
        lane = jnp.arange(LANES, dtype=jnp.int32)
        for component, tile, length in self.pieces(start, stop):
            if component is None:
                _, at, good = self.extra_unit(part, tile)
                cells.append(at * LANES + lane)
                valid.append(jnp.full((LANES,), 1.0, jnp.float32) * good.astype(jnp.float32))
            else:
                run = jnp.arange(length * LANES, dtype=jnp.int32)
                cells.append((part * self.main + tile) * LANES + run)
                valid.append(jnp.ones((length * LANES,), jnp.float32))
        return jnp.concatenate(cells), jnp.concatenate(valid)


def chunk_bounds(units):
    bounds = [0]
    for chunk in range(1, len(SHARES) + 1):
        bound = round(units * sum(SHARES[:chunk]))
        if bound > bounds[-1]:
            bounds.append(bound)
    return bounds


def split_parts(value):
    high = value.astype(jnp.bfloat16)
    low = (value - high.astype(jnp.float32)).astype(jnp.bfloat16)
    return high, low


def copies_of(parts, field_ref, part, start, stop, out_ref, sems, first_sem):
    copies = []
    for number, (component, origin, place, cells) in enumerate(parts.runs(part, start, stop)):
        copies.append(
            pltpu.make_async_copy(
                field_ref.at[:, component, :, pl.ds(origin, cells)],
                out_ref.at[:, :, pl.ds(place, cells)],
                sems.at[first_sem + number],
            )
        )
    return copies


def pack_kernel(parts, targets, start, stop, field_ref, *refs):
    outs, sems = refs[:-1], refs[-1]
    me = lax.axis_index("ka")
    copies = []
    for to, out_ref in zip(targets, outs):
        part = to(me)
        copies += copies_of(parts, field_ref, part, start, stop, out_ref, sems, len(copies))
    for copy in copies:
        copy.start()
    for copy in copies:
        copy.wait()


def pack(parts, field, targets, start, stop):
    shape = (2, field.shape[2], (stop - start) * LANES)
    anywhere = pl.BlockSpec(memory_space=pl.ANY)
    size = 4 * math.prod(shape) * len(targets)
    return pl.pallas_call(
        functools.partial(pack_kernel, parts, targets, start, stop),
        out_shape=[jax.ShapeDtypeStruct(shape, jnp.float32)] * len(targets),
        in_specs=[anywhere],
        out_specs=[pl.BlockSpec(memory_space=pltpu.VMEM)] * len(targets),
        scratch_shapes=[
            pltpu.SemaphoreType.DMA((len(targets) * len(parts.pieces(start, stop)),)),
        ],
        compiler_params=pltpu.CompilerParams(vmem_limit_bytes=4 * 1024 * 1024),
        cost_estimate=pl.CostEstimate(flops=0, bytes_accessed=2 * size, transcendentals=0),
    )(field)


def write_messages(count, offsets, factor, total_ref, out_refs, forward):
    me = lax.axis_index("ka")
    bands = total_ref.shape[1] // 2
    width = total_ref.shape[2]
    lane = lax.broadcasted_iota(jnp.int32, (bands, width), 1)
    real_lane = lane % (2 * bands) < bands
    for step in range(count):
        with_real = total_ref[step, :bands]
        with_imag = total_ref[step, bands:]
        after = pltpu.roll(with_imag, width - bands, 1)
        ahead = pltpu.roll(with_imag, bands, 1)
        forward[step] = with_real + jnp.where(real_lane, after, -ahead)
    for step in range(count):
        turn = lax.rem(step % factor + factor - lax.rem(me, factor), factor)
        group = step // factor
        back = jnp.zeros((bands, width), jnp.float32)
        for direction, offset in enumerate(offsets):
            other = forward[(step + count - offset) % count]
            back = jnp.where(lane // (2 * bands) == direction, other, back)
        for place, out_ref in enumerate(out_refs):

            @pl.when(turn == place)
            def _():
                out_ref[group, 0] = forward[step]
                out_ref[group, 1] = back


def chunk_kernel(parts, offsets, start, stop, factor, *refs):
    count = parts.count
    blocks, refs = refs[:count], refs[count:]
    (cosine_ref, sine_ref), refs = refs[:2], refs[2:]
    before_ref = None
    if start > 0:
        before_ref, refs = refs[0], refs[1:]
    last = stop == parts.units
    if last:
        outs, (held, sems, total_ref, forward) = refs[:factor], refs[factor:]
    else:
        total_ref, held, sems = refs
    me = lax.axis_index("ka")
    sources = [lambda place: place] + exchange_back(count)
    copies = [
        pltpu.make_async_copy(block, held.at[source(me)], sems.at[number])
        for number, (block, source) in enumerate(zip(blocks, sources))
    ]
    for copy in copies:
        copy.start()
    for copy in copies:
        copy.wait()

    @pl.loop(0, count)
    def _(step):
        left = held[step]
        bands, cells = left.shape[1], left.shape[2]
        left_high, left_low = split_parts(left.reshape(2 * bands, cells))
        left_rows = jnp.concatenate([left_high, left_low], axis=0)
        highs, lows = [], []
        for direction, offset in enumerate(offsets):
            right = held[lax.rem(step + offset, count)]
            cosine = cosine_ref[step * len(offsets) + direction]
            sine = sine_ref[step * len(offsets) + direction]
            w_real = cosine * right[0] - sine * right[1]
            w_imag = sine * right[0] + cosine * right[1]
            high, low = split_parts(jnp.concatenate([w_real, w_imag], axis=0))
            highs.append(high)
            lows.append(low)
        right_rows = jnp.concatenate(highs + lows, axis=0)
        product = lax.dot_general(
            left_rows,
            right_rows,
            (((1,), (1,)), ((), ())),
            preferred_element_type=jnp.float32,
        )
        half = product.shape[1] // 2
        rows = product[: 2 * bands] + product[2 * bands :]
        summed = rows[:, :half] + rows[:, half:]
        if before_ref is not None:
            summed = summed + before_ref[step]
        total_ref[step] = summed

    if last:
        write_messages(count, offsets, factor, total_ref, outs, forward)


def chunk_products(parts, blocks, cosine, sine, before, offsets, start, stop, factor):
    count = parts.count
    bands = blocks[0].shape[1]
    cells = (stop - start) * LANES
    width = 2 * len(offsets) * bands
    operands = list(blocks) + [cosine, sine]
    anywhere = pl.BlockSpec(memory_space=pl.ANY)
    inside = pl.BlockSpec(memory_space=pltpu.VMEM)
    in_specs = [anywhere] * count + [inside, inside]
    if before is not None:
        operands.append(before)
        in_specs.append(inside)
    total_shape = (count, 2 * bands, width)
    scratch = [
        pltpu.VMEM((count, 2, bands, cells), jnp.float32),
        pltpu.SemaphoreType.DMA((count,)),
    ]
    if stop == parts.units:
        message = jax.ShapeDtypeStruct((count // factor, 2, bands, width), jnp.float32)
        out_shape, out_specs = [message] * factor, [inside] * factor
        scratch += [
            pltpu.VMEM(total_shape, jnp.float32),
            pltpu.VMEM((count, bands, width), jnp.float32),
        ]
    else:
        out_shape, out_specs = jax.ShapeDtypeStruct(total_shape, jnp.float32), inside
    flops = 2 * count * (4 * bands) * (2 * width) * cells
    return pl.pallas_call(
        functools.partial(chunk_kernel, parts, offsets, start, stop, factor),
        out_shape=out_shape,
        in_specs=in_specs,
        out_specs=out_specs,
        scratch_shapes=scratch,
        compiler_params=pltpu.CompilerParams(vmem_limit_bytes=12 * 1024 * 1024),
        cost_estimate=pl.CostEstimate(
            flops=flops, bytes_accessed=4 * count * 2 * bands * cells, transcendentals=0
        ),
    )(*operands)


def block_factor(count):
    best = 1
    for factor in range(1, math.isqrt(count) + 1):
        if count % factor == 0:
            best = factor
    return best


def result_kernel(*refs):
    out_ref = refs[-1]
    total = refs[0][...]
    for ref in refs[1:-1]:
        total = total + ref[...]
    bands = out_ref.shape[2]
    flipped = total[1].T
    for direction in range(out_ref.shape[0] // 2):
        at = 2 * bands * direction
        out_ref[2 * direction, 0] = total[0, :, at : at + bands]
        out_ref[2 * direction, 1] = total[0, :, at + bands : at + 2 * bands]
        out_ref[2 * direction + 1, 0] = flipped[at : at + bands]
        out_ref[2 * direction + 1, 1] = -flipped[at + bands : at + 2 * bands]


def result(shares):
    _, bands, width = shares[0].shape
    inside = pl.BlockSpec(memory_space=pltpu.VMEM)
    return pl.pallas_call(
        result_kernel,
        out_shape=jax.ShapeDtypeStruct((width // bands, 2, bands, bands), jnp.float32),
        in_specs=[inside] * len(shares),
        out_specs=inside,
        compiler_params=pltpu.CompilerParams(vmem_limit_bytes=2 * 1024 * 1024),
    )(*shares)


def reduced_over_points(blocks, factor):
    groups = blocks[0].shape[0]
    me = lax.axis_index("ka")
    count = lax.axis_size("ka")
    total = blocks[0]
    for turn in range(1, factor):
        pairs = [
            (source, source - source % factor + (source + turn) % factor) for source in range(count)
        ]
        total = total + lax.ppermute(blocks[turn], "ka", pairs)
    group = me // factor
    mine = lax.dynamic_index_in_dim(total, group, 0, keepdims=False)
    arrived = []
    for turn in range(1, groups):
        sent = lax.dynamic_index_in_dim(total, (group + turn) % groups, 0, keepdims=False)
        arrived.append(shifted(sent, "ka", turn * factor))
    return mine + sum(arrived)


def per_device(fields, bvectors, gshift):
    count = lax.axis_size("ka")
    slabs = lax.axis_size("gz")
    me = lax.axis_index("ka")
    field = fields[0].transpose(0, 2, 1, 3)
    cells = field.shape[-1]
    plane_cells = GX * GY
    slab_depth = cells // plane_cells
    z_extent = slab_depth * slabs
    parts = Parts(field.shape[1], cells, count)
    offsets = (1 % count, KX % count)

    cell_index, valid = parts.cell_index(me, 0, parts.units)
    xcoord = (cell_index % GX).astype(jnp.float32)
    ycoord = (cell_index // GX % GY).astype(jnp.float32)
    zcoord = (lax.axis_index("gz") * slab_depth + cell_index // plane_cells).astype(jnp.float32)
    shifts_float = gshift.astype(jnp.float32)
    q_vectors = (bvectors[None] + shifts_float).reshape(-1, 3)
    angles = phase_angle(q_vectors.T[:, :, None], xcoord, ycoord, zcoord, GX, GY, z_extent)
    cosine = (jnp.cos(angles) * valid)[:, None]
    sine = (jnp.sin(angles) * valid)[:, None]

    rounds = exchange(count)
    factor = block_factor(count)
    bounds = chunk_bounds(parts.units)
    totals = []
    for chunk, (start, stop) in enumerate(zip(bounds[:-1], bounds[1:])):
        source = field
        if chunk >= AHEAD:
            source, totals[chunk - AHEAD] = lax.optimization_barrier((field, totals[chunk - AHEAD]))
        own, *sent = pack(parts, source, [lambda place: place] + rounds, start, stop)
        blocks = [own] + [sent_round(value, to) for value, to in zip(sent, rounds)]
        lanes = slice(start * LANES, stop * LANES)
        before = totals[-1] if totals else None
        totals.append(
            chunk_products(
                parts, blocks, cosine[:, :, lanes], sine[:, :, lanes], before,
                offsets, start, stop, factor,
            )
        )

    share = reduced_over_points(totals[-1], factor)
    shares = [share] + [shifted(share, "gz", step) for step in range(1, slabs)]
    return result(shares)[None]


def solution(mesh):
    in_specs = (P("ka", None, None, None, "gz"), P(), P())
    out_specs = P("ka", None, None, None, None)
    return jax.shard_map(
        per_device, mesh=mesh, in_specs=in_specs, out_specs=out_specs, check_vma=False
    )
```

```python
import functools
import math

import jax
import jax.numpy as jnp
from jax import lax
from jax.experimental import pallas as pl
from jax.experimental.pallas import tpu as pltpu
from jax.sharding import PartitionSpec as P

GX = 40
GY = 40
KX = 4
LANES = 128
SHARES = (0.37,0.37,0.26)
AHEAD = 2
EARLY = 1

two_pi = 2.0 * math.pi


def shifted(value, axis, steps):
    count = lax.axis_size(axis)
    pairs = [(source, (source + steps) % count) for source in range(count)]
    return lax.ppermute(value, axis, pairs)


def phase_angle(q_vector, xcoord, ycoord, zcoord, x_extent, y_extent, z_extent):
    return -two_pi * (
        q_vector[0] * xcoord / x_extent
        + q_vector[1] * ycoord / y_extent
        + q_vector[2] * zcoord / z_extent
    )


def exchange(count):
    turns = sorted(range(1, count), key=lambda turn: (-min(turn, count - turn), turn))
    far, near = turns[: (count + 1) // 2], turns[(count + 1) // 2 :]
    near.sort(reverse=True)
    found = []
    for place, turn in enumerate(far):
        found += [turn] + near[place : place + 1]
    return found


class Parts:
    def __init__(self, components, cells, count):
        self.components = components
        self.count = count
        tiles = cells // LANES
        self.tiles = tiles
        self.main = tiles // count
        self.rest = tiles - self.main * count
        self.extra = -(-components * self.rest // count)
        self.units = components * self.main + self.extra

    def pieces(self, start, stop):
        runs = []
        unit = start
        while unit < stop:
            if unit < self.components * self.main:
                component, tile = divmod(unit, self.main)
                length = min(self.main - tile, stop - unit)
                runs.append((component, tile, length))
            else:
                length = 1
                runs.append((None, unit - self.components * self.main, 1))
            unit += length
        return runs

    def extra_unit(self, part, slot):
        number = slot * self.count + part
        valid = number < self.components * self.rest
        number = jnp.minimum(number, self.components * self.rest - 1)
        return number // self.rest, self.main * self.count + number % self.rest, valid

    def runs(self, part, start, stop):
        found, place = [], 0
        for component, tile, length in self.pieces(start, stop):
            if component is None:
                component, at, _ = self.extra_unit(part, tile)
            else:
                at = part * self.main + tile
            found.append((component, pl.multiple_of(at * LANES, LANES), place, length * LANES))
            place += length * LANES
        return found

    def cell_index(self, part, start, stop):
        cells, valid = [], []
        lane = jnp.arange(LANES, dtype=jnp.int32)
        for component, tile, length in self.pieces(start, stop):
            if component is None:
                _, at, good = self.extra_unit(part, tile)
                cells.append(at * LANES + lane)
                valid.append(jnp.full((LANES,), 1.0, jnp.float32) * good.astype(jnp.float32))
            else:
                run = jnp.arange(length * LANES, dtype=jnp.int32)
                cells.append((part * self.main + tile) * LANES + run)
                valid.append(jnp.ones((length * LANES,), jnp.float32))
        return jnp.concatenate(cells), jnp.concatenate(valid)


def chunk_bounds(units):
    bounds = [0]
    for chunk in range(1, len(SHARES) + 1):
        bound = round(units * sum(SHARES[:chunk]))
        if bound > bounds[-1]:
            bounds.append(bound)
    return bounds


def split_parts(value):
    high = value.astype(jnp.bfloat16)
    low = (value - high.astype(jnp.float32)).astype(jnp.bfloat16)
    return high, low


def copies_of(parts, field_ref, part, start, stop, out_ref, sems, first_sem):
    copies = []
    for number, (component, origin, place, cells) in enumerate(parts.runs(part, start, stop)):
        copies.append(
            pltpu.make_async_copy(
                field_ref.at[:, component, :, pl.ds(origin, cells)],
                out_ref.at[:, :, pl.ds(place, cells)],
                sems.at[first_sem + number],
            )
        )
    return copies


def pack_kernel(parts, turns, start, stop, field_ref, *refs):
    outs, sems = refs[:-1], refs[-1]
    me = lax.axis_index("ka")
    copies = []
    for turn, out_ref in zip(turns, outs):
        part = lax.rem(me + (parts.count - turn), parts.count)
        copies += copies_of(parts, field_ref, part, start, stop, out_ref, sems, len(copies))
    for copy in copies:
        copy.start()
    for copy in copies:
        copy.wait()


def pack(parts, field, turns, start, stop, mebibytes):
    shape = (2, field.shape[2], (stop - start) * LANES)
    anywhere = pl.BlockSpec(memory_space=pl.ANY)
    size = 4 * math.prod(shape) * len(turns)
    return pl.pallas_call(
        functools.partial(pack_kernel, parts, turns, start, stop),
        out_shape=[jax.ShapeDtypeStruct(shape, jnp.float32)] * len(turns),
        in_specs=[anywhere],
        out_specs=[pl.BlockSpec(memory_space=pltpu.VMEM)] * len(turns),
        scratch_shapes=[
            pltpu.SemaphoreType.DMA((len(turns) * len(parts.pieces(start, stop)),)),
        ],
        compiler_params=pltpu.CompilerParams(vmem_limit_bytes=mebibytes * 1024 * 1024),
        cost_estimate=pl.CostEstimate(flops=0, bytes_accessed=2 * size, transcendentals=0),
    )(field)


def forward_matrices(rows):
    bands, width = rows.shape[0] // 2, rows.shape[1]
    lane = lax.broadcasted_iota(jnp.int32, (bands, width), 1)
    with_imag = rows[bands:]
    after = pltpu.roll(with_imag, width - bands, 1)
    ahead = pltpu.roll(with_imag, bands, 1)
    return rows[:bands] + jnp.where(lane % (2 * bands) < bands, after, -ahead)


def write_messages(offsets, factor, forward, out_refs):
    count = len(forward)
    me = lax.axis_index("ka")
    bands, width = forward[0].shape
    lane = lax.broadcasted_iota(jnp.int32, (bands, width), 1)
    for step in range(count):
        target = lax.rem(me + step, count)
        turn = lax.rem(lax.rem(target, factor) + factor - lax.rem(me, factor), factor)
        group = target // factor
        back = jnp.zeros((bands, width), jnp.float32)
        for direction, offset in enumerate(offsets):
            other = forward[(step + count - offset) % count]
            back = jnp.where(lane // (2 * bands) == direction, other, back)
        for place, out_ref in enumerate(out_refs):

            @pl.when(turn == place)
            def _():
                out_ref[group, 0] = forward[step]
                out_ref[group, 1] = back


def chunk_kernel(offsets, first, factor, turns, start, *refs):
    count = len(turns)
    fields = {turn: ref for turn, ref in zip(turns, refs)}
    cosine_ref, sine_ref = refs[count : count + 2]
    outs = refs[count + 2 :]
    before_ref = None
    if not first:
        before_ref, outs = outs[0], outs[1:]
    forward = []
    for step in range(count):
        left = fields[step][...]
        bands, cells = left.shape[1], left.shape[2]
        left_high, left_low = split_parts(left.reshape(2 * bands, cells))
        left_rows = jnp.concatenate([left_high, left_low], axis=0)
        highs, lows = [], []
        for direction, offset in enumerate(offsets):
            right = fields[(step + offset) % count]
            right_real, right_imag = right[0], right[1]
            row = step * len(offsets) + direction
            cosine = cosine_ref[row : row + 1, start : start + cells]
            sine = sine_ref[row : row + 1, start : start + cells]
            w_real = cosine * right_real - sine * right_imag
            w_imag = sine * right_real + cosine * right_imag
            high, low = split_parts(jnp.concatenate([w_real, w_imag], axis=0))
            highs.append(high)
            lows.append(low)
        right_rows = jnp.concatenate(highs + lows, axis=0)
        product = lax.dot_general(
            left_rows,
            right_rows,
            (((1,), (1,)), ((), ())),
            preferred_element_type=jnp.float32,
        )
        half = product.shape[1] // 2
        rows = product[: 2 * bands] + product[2 * bands :]
        summed = rows[:, :half] + rows[:, half:]
        if before_ref is not None:
            summed = summed + before_ref[step]
        if factor:
            forward.append(forward_matrices(summed))
        else:
            outs[0][step] = summed
    if factor:
        write_messages(offsets, factor, forward, outs)


def chunk_products(blocks, turns, start, cosine, sine, before, offsets, factor):
    count = len(blocks)
    _, bands, cells = blocks[0].shape
    width = 2 * len(offsets) * bands
    operands = list(blocks) + [cosine, sine]
    if before is not None:
        operands.append(before)
    inside = pl.BlockSpec(memory_space=pltpu.VMEM)
    if factor:
        message = jax.ShapeDtypeStruct((count // factor, 2, bands, width), jnp.float32)
        out_shape, out_specs = [message] * factor, [inside] * factor
    else:
        out_shape = jax.ShapeDtypeStruct((count, 2 * bands, width), jnp.float32)
        out_specs = inside
    flops = 2 * count * (4 * bands) * (2 * width) * cells
    return pl.pallas_call(
        functools.partial(chunk_kernel, offsets, before is None, factor, turns, start),
        out_shape=out_shape,
        in_specs=[inside] * len(operands),
        out_specs=out_specs,
        compiler_params=pltpu.CompilerParams(vmem_limit_bytes=16 * 1024 * 1024),
        cost_estimate=pl.CostEstimate(
            flops=flops, bytes_accessed=4 * count * 2 * bands * cells, transcendentals=0
        ),
    )(*operands)


def block_factor(count):
    return min(factor for factor in range(1, count + 1) if count % factor == 0 and factor**2 >= count)


def result_kernel(*refs):
    out_ref = refs[-1]
    total = refs[0][...]
    for ref in refs[1:-1]:
        total = total + ref[...]
    bands = out_ref.shape[2]
    flipped = total[1].T
    for direction in range(out_ref.shape[0] // 2):
        at = 2 * bands * direction
        out_ref[2 * direction, 0] = total[0, :, at : at + bands]
        out_ref[2 * direction, 1] = total[0, :, at + bands : at + 2 * bands]
        out_ref[2 * direction + 1, 0] = flipped[at : at + bands]
        out_ref[2 * direction + 1, 1] = -flipped[at + bands : at + 2 * bands]


def result(shares):
    _, bands, width = shares[0].shape
    inside = pl.BlockSpec(memory_space=pltpu.VMEM)
    return pl.pallas_call(
        result_kernel,
        out_shape=jax.ShapeDtypeStruct((width // bands, 2, bands, bands), jnp.float32),
        in_specs=[inside] * len(shares),
        out_specs=inside,
        compiler_params=pltpu.CompilerParams(vmem_limit_bytes=2 * 1024 * 1024),
    )(*shares)


def reduced_over_points(blocks, factor):
    groups = blocks[0].shape[0]
    me = lax.axis_index("ka")
    count = lax.axis_size("ka")
    total = blocks[0]
    for turn in range(1, factor):
        pairs = [
            (source, source - source % factor + (source + turn) % factor) for source in range(count)
        ]
        total = total + lax.ppermute(blocks[turn], "ka", pairs)
    group = me // factor
    mine = lax.dynamic_index_in_dim(total, group, 0, keepdims=False)
    arrived = []
    for turn in range(1, groups):
        sent = lax.dynamic_index_in_dim(total, (group + turn) % groups, 0, keepdims=False)
        arrived.append(shifted(sent, "ka", turn * factor))
    return mine + sum(arrived)


def per_device(fields, bvectors, gshift):
    count = lax.axis_size("ka")
    slabs = lax.axis_size("gz")
    me = lax.axis_index("ka")
    field = fields[0].transpose(0, 2, 1, 3)
    cells = field.shape[-1]
    plane_cells = GX * GY
    slab_depth = cells // plane_cells
    z_extent = slab_depth * slabs
    parts = Parts(field.shape[1], cells, count)
    offsets = (1 % count, KX % count)

    cell_index, valid = parts.cell_index(me, 0, parts.units)
    xcoord = (cell_index % GX).astype(jnp.float32)
    ycoord = (cell_index // GX % GY).astype(jnp.float32)
    zcoord = (lax.axis_index("gz") * slab_depth + cell_index // plane_cells).astype(jnp.float32)
    shifts_float = gshift.astype(jnp.float32)
    q_vectors = jnp.roll(bvectors[None] + shifts_float, -me, axis=0).reshape(-1, 3)
    angles = phase_angle(q_vectors.T[:, :, None], xcoord, ycoord, zcoord, GX, GY, z_extent)
    cosine = jnp.cos(angles) * valid
    sine = jnp.sin(angles) * valid

    turns = exchange(count)
    factor = block_factor(count)
    bounds = chunk_bounds(parts.units)
    totals = []
    for chunk, (start, stop) in enumerate(zip(bounds[:-1], bounds[1:])):
        source = field
        if chunk >= AHEAD:
            source, totals[chunk - AHEAD] = lax.optimization_barrier((field, totals[chunk - AHEAD]))
        early = EARLY if chunk == 0 else 0
        sent = pack(parts, source, turns[:early], start, stop, 60) if early else []
        sent += pack(parts, source, turns[early:] + [0], start, stop, 4)
        blocks = [shifted(value, "ka", -turn) for value, turn in zip(sent, turns)] + [sent[-1]]
        totals.append(
            chunk_products(
                blocks, turns + [0], start * LANES, cosine, sine,
                totals[-1] if totals else None, offsets, factor if stop == parts.units else 0,
            )
        )

    share = reduced_over_points(totals[-1], factor)
    shares = [share] + [shifted(share, "gz", step) for step in range(1, slabs)]
    return result(shares)[None]


def solution(mesh):
    in_specs = (P("ka", None, None, None, "gz"), P(), P())
    out_specs = P("ka", None, None, None, None)
    return jax.shard_map(
        per_device, mesh=mesh, in_specs=in_specs, out_specs=out_specs, check_vma=False
    )
```

```python
import functools
import math

import jax
import jax.numpy as jnp
from jax import lax
from jax.experimental import pallas as pl
from jax.experimental.pallas import tpu as pltpu
from jax.sharding import PartitionSpec as P

GX = 40
GY = 40
KX = 4
LANES = 128
SHARES = (0.37, 0.37, 0.26)
AHEAD = 2
GATE = 3
ORDERS = {8: ((2, 4, 3, 6, 7, 5, 1), (4, 7, 3, 5, 1, 2, 6), (4, 7, 3, 6, 5, 2, 1))}
FIRST = (3, 0, 1)
ROOM = 50

two_pi = 2.0 * math.pi


def shifted(value, axis, steps):
    count = lax.axis_size(axis)
    pairs = [(source, (source + steps) % count) for source in range(count)]
    return lax.ppermute(value, axis, pairs)


def phase_angle(q_vector, xcoord, ycoord, zcoord, x_extent, y_extent, z_extent):
    return -two_pi * (
        q_vector[0] * xcoord / x_extent
        + q_vector[1] * ycoord / y_extent
        + q_vector[2] * zcoord / z_extent
    )


def exchange(count):
    turns = sorted(range(1, count), key=lambda turn: (-min(turn, count - turn), turn))
    far, near = turns[: (count + 1) // 2], turns[(count + 1) // 2 :]
    near.sort(reverse=True)
    found = []
    for place, turn in enumerate(far):
        found += [turn] + near[place : place + 1]
    return found


class Parts:
    def __init__(self, components, cells, count):
        self.components = components
        self.count = count
        tiles = cells // LANES
        self.tiles = tiles
        self.main = tiles // count
        self.rest = tiles - self.main * count
        self.extra = -(-components * self.rest // count)
        self.tail = 0
        if components * self.rest * LANES % count == 0:
            share = components * self.rest * LANES // count
            if 0 < share < LANES and share % (LANES - share) == 0:
                self.tail = share
        self.units = components * self.main + self.extra

    def pieces(self, start, stop):
        runs = []
        unit = start
        while unit < stop:
            if unit < self.components * self.main:
                component, tile = divmod(unit, self.main)
                length = min(self.main - tile, stop - unit)
                runs.append((component, tile, length))
            else:
                length = 1
                runs.append((None, unit - self.components * self.main, 1))
            unit += length
        return runs

    def has_tail(self, stop):
        return self.tail > 0 and stop == self.units

    def folded(self, rows):
        return rows * self.tail // LANES

    def extra_unit(self, part, slot):
        number = slot * self.count + part
        valid = number < self.components * self.rest
        number = jnp.minimum(number, self.components * self.rest - 1)
        return number // self.rest, self.main * self.count + number % self.rest, valid

    def runs(self, part, start, stop):
        found, place = [], 0
        for component, tile, length in self.pieces(start, stop):
            if component is None:
                component, at, _ = self.extra_unit(part, tile)
            else:
                at = part * self.main + tile
            found.append((component, pl.multiple_of(at * LANES, LANES), place, length * LANES))
            place += length * LANES
        return found

    def cell_index(self, part, start, stop):
        cells, valid = [], []
        lane = jnp.arange(LANES, dtype=jnp.int32)
        for component, tile, length in self.pieces(start, stop):
            if component is None and self.tail:
                place = part * self.tail + lane
                unit = jnp.minimum(place // LANES, self.components * self.rest - 1)
                at = self.main * self.count + unit % self.rest
                cells.append(at * LANES + place % LANES)
                valid.append((lane < self.tail).astype(jnp.float32))
            elif component is None:
                _, at, good = self.extra_unit(part, tile)
                cells.append(at * LANES + lane)
                valid.append(jnp.full((LANES,), 1.0, jnp.float32) * good.astype(jnp.float32))
            else:
                run = jnp.arange(length * LANES, dtype=jnp.int32)
                cells.append((part * self.main + tile) * LANES + run)
                valid.append(jnp.ones((length * LANES,), jnp.float32))
        return jnp.concatenate(cells), jnp.concatenate(valid)


def chunk_bounds(units):
    bounds = [0]
    for chunk in range(1, len(SHARES) + 1):
        bound = round(units * sum(SHARES[:chunk]))
        if bound > bounds[-1]:
            bounds.append(bound)
    return bounds


def split_parts(value):
    high = value.astype(jnp.bfloat16)
    low = (value - high.astype(jnp.float32)).astype(jnp.bfloat16)
    return high, low


def copies_of(parts, field_ref, part, start, stop, out_ref, sems, first_sem):
    copies = []
    for number, (component, origin, place, cells) in enumerate(parts.runs(part, start, stop)):
        copies.append(
            pltpu.make_async_copy(
                field_ref.at[:, component, :, pl.ds(origin, cells)],
                out_ref.at[:, :, pl.ds(place, cells)],
                sems.at[first_sem + number],
            )
        )
    return copies


def pack_kernel(parts, turns, start, stop, field_ref, *refs):
    outs, sems = refs[:-1], refs[-1]
    me = lax.axis_index("ka")
    copies = []
    for turn, out_ref in zip(turns, outs):
        part = lax.rem(me + (parts.count - turn), parts.count)
        copies += copies_of(parts, field_ref, part, start, stop, out_ref, sems, len(copies))
    for copy in copies:
        copy.start()
    for copy in copies:
        copy.wait()


def pack(parts, field, turns, start, stop, mebibytes):
    shape = (2, field.shape[2], (stop - start) * LANES)
    anywhere = pl.BlockSpec(memory_space=pl.ANY)
    size = 4 * math.prod(shape) * len(turns)
    return pl.pallas_call(
        functools.partial(pack_kernel, parts, turns, start, stop),
        out_shape=[jax.ShapeDtypeStruct(shape, jnp.float32)] * len(turns),
        in_specs=[anywhere],
        out_specs=[pl.BlockSpec(memory_space=pltpu.VMEM)] * len(turns),
        scratch_shapes=[
            pltpu.SemaphoreType.DMA((len(turns) * len(parts.pieces(start, stop)),)),
        ],
        compiler_params=pltpu.CompilerParams(vmem_limit_bytes=mebibytes * 1024 * 1024),
        cost_estimate=pl.CostEstimate(flops=0, bytes_accessed=2 * size, transcendentals=0),
    )(field)


def fold(rows, tail):
    kept = rows.shape[0] * tail // LANES
    spare = LANES - tail
    lane = lax.broadcasted_iota(jnp.int32, (kept, LANES), 1)
    moved = [pltpu.roll(rows[kept:], tail - spare * turn, 1) for turn in range(tail // spare)]
    return jnp.where(lane < tail, rows[:kept], jnp.concatenate(moved, axis=0))


def unfold(rows, tail):
    kept = rows.shape[0]
    spare = LANES - tail
    size = kept * spare // tail
    lane = lax.broadcasted_iota(jnp.int32, (size, LANES), 1)
    last = jnp.zeros((size, LANES), jnp.float32)
    for turn in range(tail // spare):
        back = pltpu.roll(rows[turn * size : (turn + 1) * size], spare * (turn + 1), 1)
        last = jnp.where(lane // spare == turn, back, last)
    whole = jnp.concatenate([rows, last], axis=0)
    lane = lax.broadcasted_iota(jnp.int32, whole.shape, 1)
    return jnp.where(lane < tail, whole, 0.0)


def pack_tail_kernel(parts, turns, start, stop, field_ref, *refs):
    outs, (held, packed, sems) = refs[:-3], refs[-3:]
    me = lax.axis_index("ka")
    bands = field_ref.shape[2]
    first, copies = [], []

    def copy(source, target):
        sem = sems.at[len(first) + len(copies)]
        return pltpu.make_async_copy(source, target, sem)

    for unit in range(parts.components * parts.rest):
        component, tile = divmod(unit, parts.rest)
        origin = (parts.main * parts.count + tile) * LANES
        first.append(copy(field_ref.at[:, component, :, pl.ds(origin, LANES)], held.at[unit]))
    owners = [lax.rem(me + (parts.count - turn), parts.count) for turn in turns]
    for part, out_ref in zip(owners, outs):
        for unit in range(start, stop - 1):
            component, tile = divmod(unit, parts.main)
            origin = pl.multiple_of((part * parts.main + tile) * LANES, LANES)
            for half in range(2):
                rows = pl.ds((2 * (unit - start) + half) * bands, bands)
                source = field_ref.at[half, component, :, pl.ds(origin, LANES)]
                copies.append(copy(source, out_ref.at[rows]))
    for each in first + copies:
        each.start()
    for each in first:
        each.wait()
    lane = lax.broadcasted_iota(jnp.int32, (2 * bands, LANES), 1)
    for part in range(parts.count):
        unit, shift = divmod(part * parts.tail, LANES)
        rows = held[unit].reshape(2 * bands, LANES)
        if shift:
            rows = pltpu.roll(rows, LANES - shift, 1)
        if shift + parts.tail > LANES:
            after = pltpu.roll(held[unit + 1].reshape(2 * bands, LANES), LANES - shift, 1)
            rows = jnp.where(lane < LANES - shift, rows, after)
        packed[part] = fold(rows, parts.tail)
    at = 2 * bands * (stop - 1 - start)
    for part, out_ref in zip(owners, outs):
        out_ref[at:] = packed[part]
    for each in copies:
        each.wait()


def pack_tail(parts, field, turns, start, stop):
    bands = field.shape[2]
    folded = parts.folded(2 * bands)
    shape = (2 * bands * (stop - 1 - start) + folded, LANES)
    units = parts.components * parts.rest
    copies = units + 2 * len(turns) * (stop - 1 - start)
    size = 4 * math.prod(shape) * len(turns)
    return pl.pallas_call(
        functools.partial(pack_tail_kernel, parts, turns, start, stop),
        out_shape=[jax.ShapeDtypeStruct(shape, jnp.float32)] * len(turns),
        in_specs=[pl.BlockSpec(memory_space=pl.ANY)],
        out_specs=[pl.BlockSpec(memory_space=pltpu.VMEM)] * len(turns),
        scratch_shapes=[
            pltpu.VMEM((units, 2, bands, LANES), jnp.float32),
            pltpu.VMEM((parts.count, folded, LANES), jnp.float32),
            pltpu.SemaphoreType.DMA((copies,)),
        ],
        compiler_params=pltpu.CompilerParams(vmem_limit_bytes=5 * 1024 * 1024),
        cost_estimate=pl.CostEstimate(flops=0, bytes_accessed=2 * size, transcendentals=0),
    )(field)


def forward_matrices(rows):
    bands, width = rows.shape[0] // 2, rows.shape[1]
    lane = lax.broadcasted_iota(jnp.int32, (bands, width), 1)
    with_imag = rows[bands:]
    after = pltpu.roll(with_imag, width - bands, 1)
    ahead = pltpu.roll(with_imag, bands, 1)
    return rows[:bands] + jnp.where(lane % (2 * bands) < bands, after, -ahead)


def write_messages(offsets, factor, forward, out_refs):
    count = len(forward)
    me = lax.axis_index("ka")
    bands, width = forward[0].shape
    lane = lax.broadcasted_iota(jnp.int32, (bands, width), 1)
    for step in range(count):
        target = lax.rem(me + step, count)
        turn = lax.rem(lax.rem(target, factor) + factor - lax.rem(me, factor), factor)
        group = target // factor
        back = jnp.zeros((bands, width), jnp.float32)
        for direction, offset in enumerate(offsets):
            other = forward[(step + count - offset) % count]
            back = jnp.where(lane // (2 * bands) == direction, other, back)
        for place, out_ref in enumerate(out_refs):

            @pl.when(turn == place)
            def _():
                out_ref[group, 0] = forward[step]
                out_ref[group, 1] = back


def chunk_kernel(offsets, first, factor, turns, start, bands, tail, *refs):
    count = len(turns)
    fields = {turn: ref for turn, ref in zip(turns, refs)}
    cosine_ref, sine_ref = refs[count : count + 2]
    outs = refs[count + 2 :]
    before_ref = None
    if not first:
        before_ref, outs = outs[0], outs[1:]
    if tail:
        *outs, tails = outs
        at = fields[0].shape[0] // (2 * bands) * 2 * bands
        for step in range(count):
            tails[step] = unfold(fields[step][at:], tail)

    def rows_of(step):
        ref = fields[step]
        if not tail:
            return ref[...].reshape(2 * bands, ref.shape[2])
        units = [ref[row : row + 2 * bands] for row in range(0, at, 2 * bands)]
        return jnp.concatenate(units + [tails[step]], axis=1)

    forward = []
    for step in range(count):
        left_high, left_low = split_parts(rows_of(step))
        left_rows = jnp.concatenate([left_high, left_low], axis=0)
        cells = left_rows.shape[1]
        highs, lows = [], []
        for direction, offset in enumerate(offsets):
            right = rows_of((step + offset) % count)
            right_real, right_imag = right[:bands], right[bands:]
            row = step * len(offsets) + direction
            cosine = cosine_ref[row : row + 1, start : start + cells]
            sine = sine_ref[row : row + 1, start : start + cells]
            w_real = cosine * right_real - sine * right_imag
            w_imag = sine * right_real + cosine * right_imag
            high, low = split_parts(jnp.concatenate([w_real, w_imag], axis=0))
            highs.append(high)
            lows.append(low)
        right_rows = jnp.concatenate(highs + lows, axis=0)
        product = lax.dot_general(
            left_rows,
            right_rows,
            (((1,), (1,)), ((), ())),
            preferred_element_type=jnp.float32,
        )
        half = product.shape[1] // 2
        rows = product[: 2 * bands] + product[2 * bands :]
        summed = rows[:, :half] + rows[:, half:]
        if before_ref is not None:
            summed = summed + before_ref[step]
        if factor:
            forward.append(forward_matrices(summed))
        else:
            outs[0][step] = summed
    if factor:
        write_messages(offsets, factor, forward, outs)


def chunk_products(blocks, turns, start, cells, tail, cosine, sine, before, offsets, factor):
    count = len(blocks)
    bands = blocks[0].size // (2 * (cells - LANES + tail if tail else cells))
    width = 2 * len(offsets) * bands
    operands = list(blocks) + [cosine, sine]
    if before is not None:
        operands.append(before)
    inside = pl.BlockSpec(memory_space=pltpu.VMEM)
    if factor:
        message = jax.ShapeDtypeStruct((count // factor, 2, bands, width), jnp.float32)
        out_shape, out_specs = [message] * factor, [inside] * factor
    else:
        out_shape = jax.ShapeDtypeStruct((count, 2 * bands, width), jnp.float32)
        out_specs = inside
    flops = 2 * count * (4 * bands) * (2 * width) * cells
    return pl.pallas_call(
        functools.partial(chunk_kernel, offsets, before is None, factor, turns, start, bands, tail),
        out_shape=out_shape,
        in_specs=[inside] * len(operands),
        out_specs=out_specs,
        scratch_shapes=[pltpu.VMEM((count, 2 * bands, LANES), jnp.float32)] if tail else [],
        compiler_params=pltpu.CompilerParams(vmem_limit_bytes=16 * 1024 * 1024),
        cost_estimate=pl.CostEstimate(
            flops=flops, bytes_accessed=4 * count * 2 * bands * cells, transcendentals=0
        ),
    )(*operands)


def block_factor(count):
    best = 1
    for factor in range(1, math.isqrt(count) + 1):
        if count % factor == 0:
            best = factor
    return best


def result_kernel(*refs):
    out_ref = refs[-1]
    total = refs[0][...]
    for ref in refs[1:-1]:
        total = total + ref[...]
    bands = out_ref.shape[2]
    flipped = total[1].T
    for direction in range(out_ref.shape[0] // 2):
        at = 2 * bands * direction
        out_ref[2 * direction, 0] = total[0, :, at : at + bands]
        out_ref[2 * direction, 1] = total[0, :, at + bands : at + 2 * bands]
        out_ref[2 * direction + 1, 0] = flipped[at : at + bands]
        out_ref[2 * direction + 1, 1] = -flipped[at + bands : at + 2 * bands]


def result(shares):
    _, bands, width = shares[0].shape
    inside = pl.BlockSpec(memory_space=pltpu.VMEM)
    return pl.pallas_call(
        result_kernel,
        out_shape=jax.ShapeDtypeStruct((width // bands, 2, bands, bands), jnp.float32),
        in_specs=[inside] * len(shares),
        out_specs=inside,
        compiler_params=pltpu.CompilerParams(vmem_limit_bytes=2 * 1024 * 1024),
    )(*shares)


def reduced_over_points(blocks, factor):
    groups = blocks[0].shape[0]
    me = lax.axis_index("ka")
    count = lax.axis_size("ka")
    total = blocks[0]
    for turn in range(1, factor):
        pairs = [
            (source, source - source % factor + (source + turn) % factor) for source in range(count)
        ]
        total = total + lax.ppermute(blocks[turn], "ka", pairs)
    group = me // factor
    mine = lax.dynamic_index_in_dim(total, group, 0, keepdims=False)
    arrived = []
    for turn in range(1, groups):
        sent = lax.dynamic_index_in_dim(total, (group + turn) % groups, 0, keepdims=False)
        arrived.append(shifted(sent, "ka", turn * factor))
    return mine + sum(arrived)


def per_device(fields, bvectors, gshift):
    count = lax.axis_size("ka")
    slabs = lax.axis_size("gz")
    me = lax.axis_index("ka")
    field = fields[0].transpose(0, 2, 1, 3)
    cells = field.shape[-1]
    plane_cells = GX * GY
    slab_depth = cells // plane_cells
    z_extent = slab_depth * slabs
    parts = Parts(field.shape[1], cells, count)
    offsets = (1 % count, KX % count)

    cell_index, valid = parts.cell_index(me, 0, parts.units)
    xcoord = (cell_index % GX).astype(jnp.float32)
    ycoord = (cell_index // GX % GY).astype(jnp.float32)
    zcoord = (lax.axis_index("gz") * slab_depth + cell_index // plane_cells).astype(jnp.float32)
    shifts_float = gshift.astype(jnp.float32)
    q_vectors = jnp.roll(bvectors[None] + shifts_float, -me, axis=0).reshape(-1, 3)
    angles = phase_angle(q_vectors.T[:, :, None], xcoord, ycoord, zcoord, GX, GY, z_extent)
    cosine = jnp.cos(angles) * valid
    sine = jnp.sin(angles) * valid

    orders = ORDERS.get(count, [exchange(count)] * len(SHARES))
    gate = min(GATE, count - 2)
    factor = block_factor(count)
    bounds = chunk_bounds(parts.units)
    totals, blocks, extent = [], None, None

    def multiply(blocks, turns, start, stop):
        totals.append(
            chunk_products(
                blocks, turns + [0], start * LANES, (stop - start) * LANES,
                parts.tail if parts.has_tail(stop) else 0, cosine, sine,
                totals[-1] if totals else None, offsets, factor if stop == parts.units else 0,
            )
        )

    for chunk, (start, stop) in enumerate(zip(bounds[:-1], bounds[1:])):
        turns = list(orders[chunk])
        source = field
        if chunk >= AHEAD:
            source, totals[chunk - AHEAD] = lax.optimization_barrier((source, totals[chunk - AHEAD]))
        if chunk >= 1:
            source, blocks[gate] = lax.optimization_barrier((source, blocks[gate]))
            multiply(blocks, *extent)
        if parts.has_tail(stop):
            sent = pack_tail(parts, source, turns + [0], start, stop)
        else:
            first = [turns[at] for at in FIRST] if start == 0 else []
            others = [turn for turn in turns + [0] if turn not in first]
            room = 4 if start else ROOM
            found = dict(zip(first, pack(parts, source, first, start, stop, room))) if first else {}
            found.update(zip(others, pack(parts, source, others, start, stop, room)))
            sent = [found[turn] for turn in turns + [0]]
        blocks = [shifted(value, "ka", -turn) for value, turn in zip(sent, turns)] + [sent[-1]]
        extent = turns, start, stop
    multiply(blocks, *extent)

    share = reduced_over_points(totals[-1], factor)
    shares = [share] + [shifted(share, "gz", step) for step in range(1, slabs)]
    return result(shares)[None]


def solution(mesh):
    in_specs = (P("ka", None, None, None, "gz"), P(), P())
    out_specs = P("ka", None, None, None, None)
    return jax.shard_map(
        per_device, mesh=mesh, in_specs=in_specs, out_specs=out_specs, check_vma=False
    )
```

```python
import functools
import math

import jax
import jax.numpy as jnp
from jax import lax
from jax.experimental import pallas as pl
from jax.experimental.pallas import tpu as pltpu
from jax.sharding import PartitionSpec as P

GX = 40
GY = 40
KX = 4
LANES = 128
SHARES = (0.37, 0.37, 0.26)
AHEAD = 2
GATE = 3
ORDERS = {8: ((2, 4, 3, 6, 7, 5, 1), (4, 7, 3, 5, 1, 2, 6), (4, 7, 3, 6, 5, 2, 1))}
FIRST = (3, 0, 1)
ROOM = 50

two_pi = 2.0 * math.pi


def shifted(value, axis, steps):
    count = lax.axis_size(axis)
    pairs = [(source, (source + steps) % count) for source in range(count)]
    return lax.ppermute(value, axis, pairs)


def phase_angle(q_vector, xcoord, ycoord, zcoord, x_extent, y_extent, z_extent):
    return -two_pi * (
        q_vector[0] * xcoord / x_extent
        + q_vector[1] * ycoord / y_extent
        + q_vector[2] * zcoord / z_extent
    )


def exchange(count):
    turns = sorted(range(1, count), key=lambda turn: (-min(turn, count - turn), turn))
    far, near = turns[: (count + 1) // 2], turns[(count + 1) // 2 :]
    near.sort(reverse=True)
    found = []
    for place, turn in enumerate(far):
        found += [turn] + near[place : place + 1]
    return found


class Parts:
    def __init__(self, components, cells, count):
        self.components = components
        self.count = count
        tiles = cells // LANES
        self.tiles = tiles
        self.main = tiles // count
        self.rest = tiles - self.main * count
        self.extra = -(-components * self.rest // count)
        self.tail = 0
        if components * self.rest * LANES % count == 0:
            share = components * self.rest * LANES // count
            if 0 < share < LANES and share % (LANES - share) == 0:
                self.tail = share
        self.units = components * self.main + self.extra

    def pieces(self, start, stop):
        runs = []
        unit = start
        while unit < stop:
            if unit < self.components * self.main:
                component, tile = divmod(unit, self.main)
                length = min(self.main - tile, stop - unit)
                runs.append((component, tile, length))
            else:
                length = 1
                runs.append((None, unit - self.components * self.main, 1))
            unit += length
        return runs

    def has_tail(self, stop):
        return self.tail > 0 and stop == self.units

    def folded(self, rows):
        return rows * self.tail // LANES

    def extra_unit(self, part, slot):
        number = slot * self.count + part
        valid = number < self.components * self.rest
        number = jnp.minimum(number, self.components * self.rest - 1)
        return number // self.rest, self.main * self.count + number % self.rest, valid

    def runs(self, part, start, stop):
        found, place = [], 0
        for component, tile, length in self.pieces(start, stop):
            if component is None:
                component, at, _ = self.extra_unit(part, tile)
            else:
                at = part * self.main + tile
            found.append((component, pl.multiple_of(at * LANES, LANES), place, length * LANES))
            place += length * LANES
        return found

    def cell_index(self, part, start, stop):
        cells, valid = [], []
        lane = jnp.arange(LANES, dtype=jnp.int32)
        for component, tile, length in self.pieces(start, stop):
            if component is None and self.tail:
                place = part * self.tail + lane
                unit = jnp.minimum(place // LANES, self.components * self.rest - 1)
                at = self.main * self.count + unit % self.rest
                cells.append(at * LANES + place % LANES)
                valid.append((lane < self.tail).astype(jnp.float32))
            elif component is None:
                _, at, good = self.extra_unit(part, tile)
                cells.append(at * LANES + lane)
                valid.append(jnp.full((LANES,), 1.0, jnp.float32) * good.astype(jnp.float32))
            else:
                run = jnp.arange(length * LANES, dtype=jnp.int32)
                cells.append((part * self.main + tile) * LANES + run)
                valid.append(jnp.ones((length * LANES,), jnp.float32))
        return jnp.concatenate(cells), jnp.concatenate(valid)


def chunk_bounds(units):
    bounds = [0]
    for chunk in range(1, len(SHARES) + 1):
        bound = round(units * sum(SHARES[:chunk]))
        if bound > bounds[-1]:
            bounds.append(bound)
    return bounds


def split_parts(value):
    high = value.astype(jnp.bfloat16)
    low = (value - high.astype(jnp.float32)).astype(jnp.bfloat16)
    return high, low


def copies_of(parts, field_ref, part, start, stop, out_ref, sems, first_sem):
    copies = []
    for number, (component, origin, place, cells) in enumerate(parts.runs(part, start, stop)):
        copies.append(
            pltpu.make_async_copy(
                field_ref.at[:, component, :, pl.ds(origin, cells)],
                out_ref.at[:, :, pl.ds(place, cells)],
                sems.at[first_sem + number],
            )
        )
    return copies


def pack_kernel(parts, turns, start, stop, field_ref, *refs):
    outs, sems = refs[:-1], refs[-1]
    me = lax.axis_index("ka")
    copies = []
    for turn, out_ref in zip(turns, outs):
        part = lax.rem(me + (parts.count - turn), parts.count)
        copies += copies_of(parts, field_ref, part, start, stop, out_ref, sems, len(copies))
    for copy in copies:
        copy.start()
    for copy in copies:
        copy.wait()


def pack(parts, field, turns, start, stop, mebibytes):
    shape = (2, field.shape[2], (stop - start) * LANES)
    anywhere = pl.BlockSpec(memory_space=pl.ANY)
    size = 4 * math.prod(shape) * len(turns)
    return pl.pallas_call(
        functools.partial(pack_kernel, parts, turns, start, stop),
        out_shape=[jax.ShapeDtypeStruct(shape, jnp.float32)] * len(turns),
        in_specs=[anywhere],
        out_specs=[pl.BlockSpec(memory_space=pltpu.VMEM)] * len(turns),
        scratch_shapes=[
            pltpu.SemaphoreType.DMA((len(turns) * len(parts.pieces(start, stop)),)),
        ],
        compiler_params=pltpu.CompilerParams(vmem_limit_bytes=mebibytes * 1024 * 1024),
        cost_estimate=pl.CostEstimate(flops=0, bytes_accessed=2 * size, transcendentals=0),
    )(field)


def fold(rows, tail):
    kept = rows.shape[0] * tail // LANES
    spare = LANES - tail
    lane = lax.broadcasted_iota(jnp.int32, (kept, LANES), 1)
    moved = [pltpu.roll(rows[kept:], tail - spare * turn, 1) for turn in range(tail // spare)]
    return jnp.where(lane < tail, rows[:kept], jnp.concatenate(moved, axis=0))


def unfold(rows, tail):
    kept = rows.shape[0]
    spare = LANES - tail
    size = kept * spare // tail
    lane = lax.broadcasted_iota(jnp.int32, (size, LANES), 1)
    last = jnp.zeros((size, LANES), jnp.float32)
    for turn in range(tail // spare):
        back = pltpu.roll(rows[turn * size : (turn + 1) * size], spare * (turn + 1), 1)
        last = jnp.where(lane // spare == turn, back, last)
    whole = jnp.concatenate([rows, last], axis=0)
    lane = lax.broadcasted_iota(jnp.int32, whole.shape, 1)
    return jnp.where(lane < tail, whole, 0.0)


def pack_tail_kernel(parts, turns, start, stop, field_ref, *refs):
    outs, (held, packed, sems) = refs[:-3], refs[-3:]
    me = lax.axis_index("ka")
    bands = field_ref.shape[2]
    first, copies = [], []

    def copy(source, target):
        sem = sems.at[len(first) + len(copies)]
        return pltpu.make_async_copy(source, target, sem)

    for unit in range(parts.components * parts.rest):
        component, tile = divmod(unit, parts.rest)
        origin = (parts.main * parts.count + tile) * LANES
        first.append(copy(field_ref.at[:, component, :, pl.ds(origin, LANES)], held.at[unit]))
    owners = [lax.rem(me + (parts.count - turn), parts.count) for turn in turns]
    for part, out_ref in zip(owners, outs):
        for unit in range(start, stop - 1):
            component, tile = divmod(unit, parts.main)
            origin = pl.multiple_of((part * parts.main + tile) * LANES, LANES)
            for half in range(2):
                rows = pl.ds((2 * (unit - start) + half) * bands, bands)
                source = field_ref.at[half, component, :, pl.ds(origin, LANES)]
                copies.append(copy(source, out_ref.at[rows]))
    for each in first + copies:
        each.start()
    for each in first:
        each.wait()
    lane = lax.broadcasted_iota(jnp.int32, (2 * bands, LANES), 1)
    for part in range(parts.count):
        unit, shift = divmod(part * parts.tail, LANES)
        rows = held[unit].reshape(2 * bands, LANES)
        if shift:
            rows = pltpu.roll(rows, LANES - shift, 1)
        if shift + parts.tail > LANES:
            after = pltpu.roll(held[unit + 1].reshape(2 * bands, LANES), LANES - shift, 1)
            rows = jnp.where(lane < LANES - shift, rows, after)
        packed[part] = fold(rows, parts.tail)
    at = 2 * bands * (stop - 1 - start)
    for part, out_ref in zip(owners, outs):
        out_ref[at:] = packed[part]
    for each in copies:
        each.wait()


def pack_tail(parts, field, turns, start, stop):
    bands = field.shape[2]
    folded = parts.folded(2 * bands)
    shape = (2 * bands * (stop - 1 - start) + folded, LANES)
    units = parts.components * parts.rest
    copies = units + 2 * len(turns) * (stop - 1 - start)
    size = 4 * math.prod(shape) * len(turns)
    return pl.pallas_call(
        functools.partial(pack_tail_kernel, parts, turns, start, stop),
        out_shape=[jax.ShapeDtypeStruct(shape, jnp.float32)] * len(turns),
        in_specs=[pl.BlockSpec(memory_space=pl.ANY)],
        out_specs=[pl.BlockSpec(memory_space=pltpu.VMEM)] * len(turns),
        scratch_shapes=[
            pltpu.VMEM((units, 2, bands, LANES), jnp.float32),
            pltpu.VMEM((parts.count, folded, LANES), jnp.float32),
            pltpu.SemaphoreType.DMA((copies,)),
        ],
        compiler_params=pltpu.CompilerParams(vmem_limit_bytes=50 * 1024 * 1024),
        cost_estimate=pl.CostEstimate(flops=0, bytes_accessed=2 * size, transcendentals=0),
    )(field)


def forward_matrices(rows):
    bands, width = rows.shape[0] // 2, rows.shape[1]
    lane = lax.broadcasted_iota(jnp.int32, (bands, width), 1)
    with_imag = rows[bands:]
    after = pltpu.roll(with_imag, width - bands, 1)
    ahead = pltpu.roll(with_imag, bands, 1)
    return rows[:bands] + jnp.where(lane % (2 * bands) < bands, after, -ahead)


def write_messages(offsets, factor, forward, out_refs):
    count = len(forward)
    me = lax.axis_index("ka")
    bands, width = forward[0].shape
    lane = lax.broadcasted_iota(jnp.int32, (bands, width), 1)
    for step in range(count):
        target = lax.rem(me + step, count)
        turn = lax.rem(lax.rem(target, factor) + factor - lax.rem(me, factor), factor)
        group = target // factor
        back = jnp.zeros((bands, width), jnp.float32)
        for direction, offset in enumerate(offsets):
            other = forward[(step + count - offset) % count]
            back = jnp.where(lane // (2 * bands) == direction, other, back)
        for place, out_ref in enumerate(out_refs):

            @pl.when(turn == place)
            def _():
                out_ref[group, 0] = forward[step]
                out_ref[group, 1] = back


def chunk_kernel(offsets, first, factor, turns, start, bands, tail, *refs):
    count = len(turns)
    fields = {turn: ref for turn, ref in zip(turns, refs)}
    cosine_ref, sine_ref = refs[count : count + 2]
    outs = refs[count + 2 :]
    before_ref = None
    if not first:
        before_ref, outs = outs[0], outs[1:]
    if tail:
        *outs, tails = outs
        at = fields[0].shape[0] // (2 * bands) * 2 * bands
        for step in range(count):
            tails[step] = unfold(fields[step][at:], tail)

    def rows_of(step):
        ref = fields[step]
        if not tail:
            return ref[...].reshape(2 * bands, ref.shape[2])
        units = [ref[row : row + 2 * bands] for row in range(0, at, 2 * bands)]
        return jnp.concatenate(units + [tails[step]], axis=1)

    forward = []
    for step in range(count):
        left_high, left_low = split_parts(rows_of(step))
        left_rows = jnp.concatenate([left_high, left_low], axis=0)
        cells = left_rows.shape[1]
        highs, lows = [], []
        for direction, offset in enumerate(offsets):
            right = rows_of((step + offset) % count)
            right_real, right_imag = right[:bands], right[bands:]
            row = step * len(offsets) + direction
            cosine = cosine_ref[row : row + 1, start : start + cells]
            sine = sine_ref[row : row + 1, start : start + cells]
            w_real = cosine * right_real - sine * right_imag
            w_imag = sine * right_real + cosine * right_imag
            high, low = split_parts(jnp.concatenate([w_real, w_imag], axis=0))
            highs.append(high)
            lows.append(low)
        right_rows = jnp.concatenate(highs + lows, axis=0)
        product = lax.dot_general(
            left_rows,
            right_rows,
            (((1,), (1,)), ((), ())),
            preferred_element_type=jnp.float32,
        )
        half = product.shape[1] // 2
        rows = product[: 2 * bands] + product[2 * bands :]
        summed = rows[:, :half] + rows[:, half:]
        if before_ref is not None:
            summed = summed + before_ref[step]
        if factor:
            forward.append(forward_matrices(summed))
        else:
            outs[0][step] = summed
    if factor:
        write_messages(offsets, factor, forward, outs)


def chunk_products(blocks, turns, start, cells, tail, cosine, sine, before, offsets, factor):
    count = len(blocks)
    bands = blocks[0].size // (2 * (cells - LANES + tail if tail else cells))
    width = 2 * len(offsets) * bands
    operands = list(blocks) + [cosine, sine]
    if before is not None:
        operands.append(before)
    inside = pl.BlockSpec(memory_space=pltpu.VMEM)
    if factor:
        message = jax.ShapeDtypeStruct((count // factor, 2, bands, width), jnp.float32)
        out_shape, out_specs = [message] * factor, [inside] * factor
    else:
        out_shape = jax.ShapeDtypeStruct((count, 2 * bands, width), jnp.float32)
        out_specs = inside
    flops = 2 * count * (4 * bands) * (2 * width) * cells
    return pl.pallas_call(
        functools.partial(chunk_kernel, offsets, before is None, factor, turns, start, bands, tail),
        out_shape=out_shape,
        in_specs=[inside] * len(operands),
        out_specs=out_specs,
        scratch_shapes=[pltpu.VMEM((count, 2 * bands, LANES), jnp.float32)] if tail else [],
        compiler_params=pltpu.CompilerParams(vmem_limit_bytes=16 * 1024 * 1024),
        cost_estimate=pl.CostEstimate(
            flops=flops, bytes_accessed=4 * count * 2 * bands * cells, transcendentals=0
        ),
    )(*operands)


def block_factor(count):
    best = 1
    for factor in range(1, math.isqrt(count) + 1):
        if count % factor == 0:
            best = factor
    return best


def result_kernel(*refs):
    out_ref = refs[-1]
    total = refs[0][...]
    for ref in refs[1:-1]:
        total = total + ref[...]
    bands = out_ref.shape[2]
    flipped = total[1].T
    for direction in range(out_ref.shape[0] // 2):
        at = 2 * bands * direction
        out_ref[2 * direction, 0] = total[0, :, at : at + bands]
        out_ref[2 * direction, 1] = total[0, :, at + bands : at + 2 * bands]
        out_ref[2 * direction + 1, 0] = flipped[at : at + bands]
        out_ref[2 * direction + 1, 1] = -flipped[at + bands : at + 2 * bands]


def result(shares):
    _, bands, width = shares[0].shape
    inside = pl.BlockSpec(memory_space=pltpu.VMEM)
    return pl.pallas_call(
        result_kernel,
        out_shape=jax.ShapeDtypeStruct((width // bands, 2, bands, bands), jnp.float32),
        in_specs=[inside] * len(shares),
        out_specs=inside,
        compiler_params=pltpu.CompilerParams(vmem_limit_bytes=2 * 1024 * 1024),
    )(*shares)


def reduced_over_points(blocks, factor):
    groups = blocks[0].shape[0]
    me = lax.axis_index("ka")
    count = lax.axis_size("ka")
    total = blocks[0]
    for turn in range(1, factor):
        pairs = [
            (source, source - source % factor + (source + turn) % factor) for source in range(count)
        ]
        total = total + lax.ppermute(blocks[turn], "ka", pairs)
    group = me // factor
    mine = lax.dynamic_index_in_dim(total, group, 0, keepdims=False)
    arrived = []
    for turn in range(1, groups):
        sent = lax.dynamic_index_in_dim(total, (group + turn) % groups, 0, keepdims=False)
        arrived.append(shifted(sent, "ka", turn * factor))
    return mine + sum(arrived)


def per_device(fields, bvectors, gshift):
    count = lax.axis_size("ka")
    slabs = lax.axis_size("gz")
    me = lax.axis_index("ka")
    field = fields[0].transpose(0, 2, 1, 3)
    cells = field.shape[-1]
    plane_cells = GX * GY
    slab_depth = cells // plane_cells
    z_extent = slab_depth * slabs
    parts = Parts(field.shape[1], cells, count)
    offsets = (1 % count, KX % count)

    cell_index, valid = parts.cell_index(me, 0, parts.units)
    xcoord = (cell_index % GX).astype(jnp.float32)
    ycoord = (cell_index // GX % GY).astype(jnp.float32)
    zcoord = (lax.axis_index("gz") * slab_depth + cell_index // plane_cells).astype(jnp.float32)
    shifts_float = gshift.astype(jnp.float32)
    q_vectors = jnp.roll(bvectors[None] + shifts_float, -me, axis=0).reshape(-1, 3)
    angles = phase_angle(q_vectors.T[:, :, None], xcoord, ycoord, zcoord, GX, GY, z_extent)
    cosine = jnp.cos(angles) * valid
    sine = jnp.sin(angles) * valid

    orders = ORDERS.get(count, [exchange(count)] * len(SHARES))
    gate = min(GATE, count - 2)
    factor = block_factor(count)
    bounds = chunk_bounds(parts.units)
    totals, blocks, extent = [], None, None

    def multiply(blocks, turns, start, stop):
        totals.append(
            chunk_products(
                blocks, turns + [0], start * LANES, (stop - start) * LANES,
                parts.tail if parts.has_tail(stop) else 0, cosine, sine,
                totals[-1] if totals else None, offsets, factor if stop == parts.units else 0,
            )
        )

    for chunk, (start, stop) in enumerate(zip(bounds[:-1], bounds[1:])):
        turns = list(orders[chunk])
        source = field
        if chunk >= AHEAD:
            source, totals[chunk - AHEAD] = lax.optimization_barrier((source, totals[chunk - AHEAD]))
        if chunk >= 1:
            source, blocks[gate] = lax.optimization_barrier((source, blocks[gate]))
            multiply(blocks, *extent)
        if parts.has_tail(stop):
            sent = pack_tail(parts, source, turns + [0], start, stop)
        else:
            first = [turns[at] for at in FIRST] if start == 0 else []
            others = [turn for turn in turns + [0] if turn not in first]
            room = ROOM
            found = dict(zip(first, pack(parts, source, first, start, stop, room))) if first else {}
            found.update(zip(others, pack(parts, source, others, start, stop, room)))
            sent = [found[turn] for turn in turns + [0]]
        blocks = [shifted(value, "ka", -turn) for value, turn in zip(sent, turns)] + [sent[-1]]
        extent = turns, start, stop
    multiply(blocks, *extent)

    share = reduced_over_points(totals[-1], factor)
    shares = [share] + [shifted(share, "gz", step) for step in range(1, slabs)]
    return result(shares)[None]


def solution(mesh):
    in_specs = (P("ka", None, None, None, "gz"), P(), P())
    out_specs = P("ka", None, None, None, None)
    return jax.shard_map(
        per_device, mesh=mesh, in_specs=in_specs, out_specs=out_specs, check_vma=False
    )
```

```python
import functools
import math

import jax
import jax.numpy as jnp
from jax import lax
from jax.experimental import pallas as pl
from jax.experimental.pallas import tpu as pltpu
from jax.sharding import PartitionSpec as P

GX = 40
GY = 40
KX = 4
LANES = 128
SHARES = (0.37, 0.37, 0.26)
AHEAD = 2
GATE = 3
ORDERS = {8: ((2, 4, 3, 6, 7, 5, 1), (4, 7, 3, 5, 1, 2, 6), (4, 7, 3, 6, 5, 2, 1))}
FIRST = (3, 0, 1)
ROOM = 50

two_pi = 2.0 * math.pi


def shifted(value, axis, steps):
    count = lax.axis_size(axis)
    pairs = [(source, (source + steps) % count) for source in range(count)]
    return lax.ppermute(value, axis, pairs)


def swapped(value, axis, turn):
    count = lax.axis_size(axis)
    if count & (count - 1):
        return shifted(value, axis, turn)
    return lax.ppermute(value, axis, [(source, source ^ turn) for source in range(count)])


def far_first(count):
    half = (count + 1) // 2
    return list(range(half, count)) + list(range(1, half))


def phase_angle(q_vector, xcoord, ycoord, zcoord, x_extent, y_extent, z_extent):
    return -two_pi * (
        q_vector[0] * xcoord / x_extent
        + q_vector[1] * ycoord / y_extent
        + q_vector[2] * zcoord / z_extent
    )


def exchange(count):
    turns = sorted(range(1, count), key=lambda turn: (-min(turn, count - turn), turn))
    far, near = turns[: (count + 1) // 2], turns[(count + 1) // 2 :]
    near.sort(reverse=True)
    found = []
    for place, turn in enumerate(far):
        found += [turn] + near[place : place + 1]
    return found


class Parts:
    def __init__(self, components, cells, count):
        self.components = components
        self.count = count
        tiles = cells // LANES
        self.tiles = tiles
        self.main = tiles // count
        self.rest = tiles - self.main * count
        self.extra = -(-components * self.rest // count)
        self.tail = 0
        if components * self.rest * LANES % count == 0:
            share = components * self.rest * LANES // count
            if 0 < share < LANES and share % (LANES - share) == 0:
                self.tail = share
        self.units = components * self.main + self.extra

    def pieces(self, start, stop):
        runs = []
        unit = start
        while unit < stop:
            if unit < self.components * self.main:
                component, tile = divmod(unit, self.main)
                length = min(self.main - tile, stop - unit)
                runs.append((component, tile, length))
            else:
                length = 1
                runs.append((None, unit - self.components * self.main, 1))
            unit += length
        return runs

    def has_tail(self, stop):
        return self.tail > 0 and stop == self.units

    def folded(self, rows):
        return rows * self.tail // LANES

    def extra_unit(self, part, slot):
        number = slot * self.count + part
        valid = number < self.components * self.rest
        number = jnp.minimum(number, self.components * self.rest - 1)
        return number // self.rest, self.main * self.count + number % self.rest, valid

    def runs(self, part, start, stop):
        found, place = [], 0
        for component, tile, length in self.pieces(start, stop):
            if component is None:
                component, at, _ = self.extra_unit(part, tile)
            else:
                at = part * self.main + tile
            found.append((component, pl.multiple_of(at * LANES, LANES), place, length * LANES))
            place += length * LANES
        return found

    def cell_index(self, part, start, stop):
        cells, valid = [], []
        lane = jnp.arange(LANES, dtype=jnp.int32)
        for component, tile, length in self.pieces(start, stop):
            if component is None and self.tail:
                place = part * self.tail + lane
                unit = jnp.minimum(place // LANES, self.components * self.rest - 1)
                at = self.main * self.count + unit % self.rest
                cells.append(at * LANES + place % LANES)
                valid.append((lane < self.tail).astype(jnp.float32))
            elif component is None:
                _, at, good = self.extra_unit(part, tile)
                cells.append(at * LANES + lane)
                valid.append(jnp.full((LANES,), 1.0, jnp.float32) * good.astype(jnp.float32))
            else:
                run = jnp.arange(length * LANES, dtype=jnp.int32)
                cells.append((part * self.main + tile) * LANES + run)
                valid.append(jnp.ones((length * LANES,), jnp.float32))
        return jnp.concatenate(cells), jnp.concatenate(valid)


def chunk_bounds(units):
    bounds = [0]
    for chunk in range(1, len(SHARES) + 1):
        bound = round(units * sum(SHARES[:chunk]))
        if bound > bounds[-1]:
            bounds.append(bound)
    return bounds


def split_parts(value):
    high = value.astype(jnp.bfloat16)
    low = (value - high.astype(jnp.float32)).astype(jnp.bfloat16)
    return high, low


def copies_of(parts, field_ref, part, start, stop, out_ref, sems, first_sem):
    copies = []
    for number, (component, origin, place, cells) in enumerate(parts.runs(part, start, stop)):
        copies.append(
            pltpu.make_async_copy(
                field_ref.at[:, component, :, pl.ds(origin, cells)],
                out_ref.at[:, :, pl.ds(place, cells)],
                sems.at[first_sem + number],
            )
        )
    return copies


def pack_kernel(parts, turns, start, stop, field_ref, *refs):
    outs, sems = refs[:-1], refs[-1]
    me = lax.axis_index("ka")
    copies = []
    for turn, out_ref in zip(turns, outs):
        part = lax.rem(me + (parts.count - turn), parts.count)
        copies += copies_of(parts, field_ref, part, start, stop, out_ref, sems, len(copies))
    for copy in copies:
        copy.start()
    for copy in copies:
        copy.wait()


def pack(parts, field, turns, start, stop, mebibytes):
    shape = (2, field.shape[2], (stop - start) * LANES)
    anywhere = pl.BlockSpec(memory_space=pl.ANY)
    size = 4 * math.prod(shape) * len(turns)
    return pl.pallas_call(
        functools.partial(pack_kernel, parts, turns, start, stop),
        out_shape=[jax.ShapeDtypeStruct(shape, jnp.float32)] * len(turns),
        in_specs=[anywhere],
        out_specs=[pl.BlockSpec(memory_space=pltpu.VMEM)] * len(turns),
        scratch_shapes=[
            pltpu.SemaphoreType.DMA((len(turns) * len(parts.pieces(start, stop)),)),
        ],
        compiler_params=pltpu.CompilerParams(vmem_limit_bytes=mebibytes * 1024 * 1024),
        cost_estimate=pl.CostEstimate(flops=0, bytes_accessed=2 * size, transcendentals=0),
    )(field)


def fold(rows, tail):
    kept = rows.shape[0] * tail // LANES
    spare = LANES - tail
    lane = lax.broadcasted_iota(jnp.int32, (kept, LANES), 1)
    moved = [pltpu.roll(rows[kept:], tail - spare * turn, 1) for turn in range(tail // spare)]
    return jnp.where(lane < tail, rows[:kept], jnp.concatenate(moved, axis=0))


def unfold(rows, tail):
    kept = rows.shape[0]
    spare = LANES - tail
    size = kept * spare // tail
    lane = lax.broadcasted_iota(jnp.int32, (size, LANES), 1)
    last = jnp.zeros((size, LANES), jnp.float32)
    for turn in range(tail // spare):
        back = pltpu.roll(rows[turn * size : (turn + 1) * size], spare * (turn + 1), 1)
        last = jnp.where(lane // spare == turn, back, last)
    whole = jnp.concatenate([rows, last], axis=0)
    lane = lax.broadcasted_iota(jnp.int32, whole.shape, 1)
    return jnp.where(lane < tail, whole, 0.0)


def pack_tail_kernel(parts, turns, start, stop, field_ref, *refs):
    outs, (held, packed, sems) = refs[:-3], refs[-3:]
    me = lax.axis_index("ka")
    bands = field_ref.shape[2]
    first, copies = [], []

    def copy(source, target):
        sem = sems.at[len(first) + len(copies)]
        return pltpu.make_async_copy(source, target, sem)

    for unit in range(parts.components * parts.rest):
        component, tile = divmod(unit, parts.rest)
        origin = (parts.main * parts.count + tile) * LANES
        first.append(copy(field_ref.at[:, component, :, pl.ds(origin, LANES)], held.at[unit]))
    owners = [lax.rem(me + (parts.count - turn), parts.count) for turn in turns]
    for part, out_ref in zip(owners, outs):
        for unit in range(start, stop - 1):
            component, tile = divmod(unit, parts.main)
            origin = pl.multiple_of((part * parts.main + tile) * LANES, LANES)
            for half in range(2):
                rows = pl.ds((2 * (unit - start) + half) * bands, bands)
                source = field_ref.at[half, component, :, pl.ds(origin, LANES)]
                copies.append(copy(source, out_ref.at[rows]))
    for each in first + copies:
        each.start()
    for each in first:
        each.wait()
    lane = lax.broadcasted_iota(jnp.int32, (2 * bands, LANES), 1)
    for part in range(parts.count):
        unit, shift = divmod(part * parts.tail, LANES)
        rows = held[unit].reshape(2 * bands, LANES)
        if shift:
            rows = pltpu.roll(rows, LANES - shift, 1)
        if shift + parts.tail > LANES:
            after = pltpu.roll(held[unit + 1].reshape(2 * bands, LANES), LANES - shift, 1)
            rows = jnp.where(lane < LANES - shift, rows, after)
        packed[part] = fold(rows, parts.tail)
    at = 2 * bands * (stop - 1 - start)
    for part, out_ref in zip(owners, outs):
        out_ref[at:] = packed[part]
    for each in copies:
        each.wait()


def pack_tail(parts, field, turns, start, stop):
    bands = field.shape[2]
    folded = parts.folded(2 * bands)
    shape = (2 * bands * (stop - 1 - start) + folded, LANES)
    units = parts.components * parts.rest
    copies = units + 2 * len(turns) * (stop - 1 - start)
    size = 4 * math.prod(shape) * len(turns)
    return pl.pallas_call(
        functools.partial(pack_tail_kernel, parts, turns, start, stop),
        out_shape=[jax.ShapeDtypeStruct(shape, jnp.float32)] * len(turns),
        in_specs=[pl.BlockSpec(memory_space=pl.ANY)],
        out_specs=[pl.BlockSpec(memory_space=pltpu.VMEM)] * len(turns),
        scratch_shapes=[
            pltpu.VMEM((units, 2, bands, LANES), jnp.float32),
            pltpu.VMEM((parts.count, folded, LANES), jnp.float32),
            pltpu.SemaphoreType.DMA((copies,)),
        ],
        compiler_params=pltpu.CompilerParams(vmem_limit_bytes=50 * 1024 * 1024),
        cost_estimate=pl.CostEstimate(flops=0, bytes_accessed=2 * size, transcendentals=0),
    )(field)


def forward_matrices(rows):
    bands, width = rows.shape[0] // 2, rows.shape[1]
    lane = lax.broadcasted_iota(jnp.int32, (bands, width), 1)
    with_imag = rows[bands:]
    after = pltpu.roll(with_imag, width - bands, 1)
    ahead = pltpu.roll(with_imag, bands, 1)
    return rows[:bands] + jnp.where(lane % (2 * bands) < bands, after, -ahead)


def write_messages(offsets, factor, forward, out_refs):
    count = len(forward)
    me = lax.axis_index("ka")
    bands, width = forward[0].shape
    lane = lax.broadcasted_iota(jnp.int32, (bands, width), 1)
    for step in range(count):
        target = lax.rem(me + step, count)
        turn = lax.rem(lax.rem(target, factor) + factor - lax.rem(me, factor), factor)
        group = target // factor
        back = jnp.zeros((bands, width), jnp.float32)
        for direction, offset in enumerate(offsets):
            other = forward[(step + count - offset) % count]
            back = jnp.where(lane // (2 * bands) == direction, other, back)
        for place, out_ref in enumerate(out_refs):

            @pl.when(turn == place)
            def _():
                out_ref[group, 0] = forward[step]
                out_ref[group, 1] = back


def chunk_kernel(offsets, first, factor, turns, start, bands, tail, *refs):
    count = len(turns)
    fields = {turn: ref for turn, ref in zip(turns, refs)}
    cosine_ref, sine_ref = refs[count : count + 2]
    outs = refs[count + 2 :]
    before_ref = None
    if not first:
        before_ref, outs = outs[0], outs[1:]
    if tail:
        *outs, tails = outs
        at = fields[0].shape[0] // (2 * bands) * 2 * bands
        for step in range(count):
            tails[step] = unfold(fields[step][at:], tail)

    def rows_of(step):
        ref = fields[step]
        if not tail:
            return ref[...].reshape(2 * bands, ref.shape[2])
        units = [ref[row : row + 2 * bands] for row in range(0, at, 2 * bands)]
        return jnp.concatenate(units + [tails[step]], axis=1)

    forward = []
    for step in range(count):
        left_high, left_low = split_parts(rows_of(step))
        left_rows = jnp.concatenate([left_high, left_low], axis=0)
        cells = left_rows.shape[1]
        highs, lows = [], []
        for direction, offset in enumerate(offsets):
            right = rows_of((step + offset) % count)
            right_real, right_imag = right[:bands], right[bands:]
            row = step * len(offsets) + direction
            cosine = cosine_ref[row : row + 1, start : start + cells]
            sine = sine_ref[row : row + 1, start : start + cells]
            w_real = cosine * right_real - sine * right_imag
            w_imag = sine * right_real + cosine * right_imag
            high, low = split_parts(jnp.concatenate([w_real, w_imag], axis=0))
            highs.append(high)
            lows.append(low)
        right_rows = jnp.concatenate(highs + lows, axis=0)
        product = lax.dot_general(
            left_rows,
            right_rows,
            (((1,), (1,)), ((), ())),
            preferred_element_type=jnp.float32,
        )
        half = product.shape[1] // 2
        rows = product[: 2 * bands] + product[2 * bands :]
        summed = rows[:, :half] + rows[:, half:]
        if before_ref is not None:
            summed = summed + before_ref[step]
        if factor:
            forward.append(forward_matrices(summed))
        else:
            outs[0][step] = summed
    if factor:
        write_messages(offsets, factor, forward, outs)


def chunk_products(blocks, turns, start, cells, tail, cosine, sine, before, offsets, factor):
    count = len(blocks)
    bands = blocks[0].size // (2 * (cells - LANES + tail if tail else cells))
    width = 2 * len(offsets) * bands
    operands = list(blocks) + [cosine, sine]
    if before is not None:
        operands.append(before)
    inside = pl.BlockSpec(memory_space=pltpu.VMEM)
    if factor:
        message = jax.ShapeDtypeStruct((count // factor, 2, bands, width), jnp.float32)
        out_shape, out_specs = [message] * factor, [inside] * factor
    else:
        out_shape = jax.ShapeDtypeStruct((count, 2 * bands, width), jnp.float32)
        out_specs = inside
    flops = 2 * count * (4 * bands) * (2 * width) * cells
    return pl.pallas_call(
        functools.partial(chunk_kernel, offsets, before is None, factor, turns, start, bands, tail),
        out_shape=out_shape,
        in_specs=[inside] * len(operands),
        out_specs=out_specs,
        scratch_shapes=[pltpu.VMEM((count, 2 * bands, LANES), jnp.float32)] if tail else [],
        compiler_params=pltpu.CompilerParams(vmem_limit_bytes=16 * 1024 * 1024),
        cost_estimate=pl.CostEstimate(
            flops=flops, bytes_accessed=4 * count * 2 * bands * cells, transcendentals=0
        ),
    )(*operands)


def block_factor(count):
    best = 1
    for factor in range(1, math.isqrt(count) + 1):
        if count % factor == 0:
            best = factor
    return best


def result_kernel(*refs):
    out_ref = refs[-1]
    total = refs[0][...]
    for ref in refs[1:-1]:
        total = total + ref[...]
    bands = out_ref.shape[2]
    flipped = total[1].T
    for direction in range(out_ref.shape[0] // 2):
        at = 2 * bands * direction
        out_ref[2 * direction, 0] = total[0, :, at : at + bands]
        out_ref[2 * direction, 1] = total[0, :, at + bands : at + 2 * bands]
        out_ref[2 * direction + 1, 0] = flipped[at : at + bands]
        out_ref[2 * direction + 1, 1] = -flipped[at + bands : at + 2 * bands]


def result(shares):
    _, bands, width = shares[0].shape
    inside = pl.BlockSpec(memory_space=pltpu.VMEM)
    return pl.pallas_call(
        result_kernel,
        out_shape=jax.ShapeDtypeStruct((width // bands, 2, bands, bands), jnp.float32),
        in_specs=[inside] * len(shares),
        out_specs=inside,
        compiler_params=pltpu.CompilerParams(vmem_limit_bytes=2 * 1024 * 1024),
    )(*shares)


def reduced_over_points(blocks, factor):
    groups = blocks[0].shape[0]
    me = lax.axis_index("ka")
    count = lax.axis_size("ka")
    total = blocks[0]
    for turn in range(1, factor):
        pairs = [
            (source, source - source % factor + (source + turn) % factor) for source in range(count)
        ]
        total = total + lax.ppermute(blocks[turn], "ka", pairs)
    group = me // factor
    mine = lax.dynamic_index_in_dim(total, group, 0, keepdims=False)
    arrived = []
    for turn in range(1, groups):
        sent = lax.dynamic_index_in_dim(total, (group + turn) % groups, 0, keepdims=False)
        arrived.append(shifted(sent, "ka", turn * factor))
    return mine + sum(arrived)


def per_device(fields, bvectors, gshift):
    count = lax.axis_size("ka")
    slabs = lax.axis_size("gz")
    me = lax.axis_index("ka")
    field = fields[0].transpose(0, 2, 1, 3)
    cells = field.shape[-1]
    plane_cells = GX * GY
    slab_depth = cells // plane_cells
    z_extent = slab_depth * slabs
    parts = Parts(field.shape[1], cells, count)
    offsets = (1 % count, KX % count)

    cell_index, valid = parts.cell_index(me, 0, parts.units)
    xcoord = (cell_index % GX).astype(jnp.float32)
    ycoord = (cell_index // GX % GY).astype(jnp.float32)
    zcoord = (lax.axis_index("gz") * slab_depth + cell_index // plane_cells).astype(jnp.float32)
    shifts_float = gshift.astype(jnp.float32)
    q_vectors = jnp.roll(bvectors[None] + shifts_float, -me, axis=0).reshape(-1, 3)
    angles = phase_angle(q_vectors.T[:, :, None], xcoord, ycoord, zcoord, GX, GY, z_extent)
    cosine = jnp.cos(angles) * valid
    sine = jnp.sin(angles) * valid

    orders = ORDERS.get(count, [exchange(count)] * len(SHARES))
    gate = min(GATE, count - 2)
    factor = block_factor(count)
    bounds = chunk_bounds(parts.units)
    totals, blocks, extent = [], None, None

    def multiply(blocks, turns, start, stop):
        totals.append(
            chunk_products(
                blocks, turns + [0], start * LANES, (stop - start) * LANES,
                parts.tail if parts.has_tail(stop) else 0, cosine, sine,
                totals[-1] if totals else None, offsets, factor if stop == parts.units else 0,
            )
        )

    for chunk, (start, stop) in enumerate(zip(bounds[:-1], bounds[1:])):
        turns = list(orders[chunk])
        source = field
        if chunk >= AHEAD:
            source, totals[chunk - AHEAD] = lax.optimization_barrier((source, totals[chunk - AHEAD]))
        if chunk >= 1:
            source, blocks[gate] = lax.optimization_barrier((source, blocks[gate]))
            multiply(blocks, *extent)
        if parts.has_tail(stop):
            sent = pack_tail(parts, source, turns + [0], start, stop)
        else:
            first = [turns[at] for at in FIRST] if start == 0 else []
            others = [turn for turn in turns + [0] if turn not in first]
            room = ROOM
            found = dict(zip(first, pack(parts, source, first, start, stop, room))) if first else {}
            found.update(zip(others, pack(parts, source, others, start, stop, room)))
            sent = [found[turn] for turn in turns + [0]]
        blocks = [shifted(value, "ka", -turn) for value, turn in zip(sent, turns)] + [sent[-1]]
        extent = turns, start, stop
    multiply(blocks, *extent)

    share = reduced_over_points(totals[-1], factor)
    shares = [share] + [swapped(share, "gz", step) for step in far_first(slabs)]
    return result(shares)[None]


def solution(mesh):
    in_specs = (P("ka", None, None, None, "gz"), P(), P())
    out_specs = P("ka", None, None, None, None)
    return jax.shard_map(
        per_device, mesh=mesh, in_specs=in_specs, out_specs=out_specs, check_vma=False
    )
```
